32 devices in a mesh: grp: 2 (over x), seq: 16 (over z, y, core).
Axes of the slice: x: 2, y: 2, z: 4, core: 2. Of those that a mesh axis runs over, the one named last changes fastest.
Arguments:
- projected: bfloat16 [3, 4096, 4096], P(None, ('grp', 'seq')), parts along dimension 1, may hold values from -6 to 6
- short_taps: float32 [3, 3, 4096], replicated, may hold values from -3 to 3
- skip_gain: float32 [4096], replicated, may hold values from -3 to 3
- residues: float32 [2, 2, 4096], replicated, may hold values from -0.125 to 0.125
- pole_angles: float32 [2, 4096], replicated, may hold values from -3.140625 to 3.140625
- decay_rates: float32 [2, 4096], replicated, may hold values from 3.0517578e-05 to 0.03125
Outputs:
- gated: bfloat16 [4096, 4096], P(('grp', 'seq')), parts along dimension 0
The draws below stay inside these ranges and needn't reach their ends.
There are 2 independent parts, one for each index of `grp`. The reference program is written for one: setup_inputs(seed, part) draws one part's arguments, and reference() takes and returns one part's arrays. A program takes and returns all parts, laid end to end along the dimension named above; an argument that names none is the same for every part. Nothing has to cross between parts.
All inputs are finite; a program needn't handle non-finite values.
Results may differ from the reference program's by a relative error of at most 0.008.
Values may be sent and summed in bfloat16 or wider, within the bound.
A program may use at most 128 MiB of HBM per device.

```python
import math
import jax
import jax.numpy as jnp
from jax import lax

D = 4096
STATE = 2
SHORT = 3
LENGTH = 2048


def draw_decay_rates(key, part):
    pick_key, slow_key, fast_key = jax.random.split(key, 3)
    chooser = jax.random.uniform(pick_key, (STATE, D), jnp.float32)
    slow_rate = jnp.exp(jax.random.uniform(slow_key, (STATE, D), jnp.float32, math.log(0.3 / LENGTH), math.log(2.0 / LENGTH)))
    fast_rate = jnp.exp(jax.random.uniform(fast_key, (STATE, D), jnp.float32, math.log(1.0 / 400.0), math.log(0.99 / 32.0)))
    share = 0.5
    return jnp.where(chooser < share, slow_rate, fast_rate)


def level_of(own_key, extent, cuts, smallest, high):
    gain = 1.0
    for axis_at, shards_of in cuts:
        heights = jax.random.uniform(jax.random.fold_in(jax.random.fold_in(own_key, 6), axis_at), (shards_of,), jnp.float32, smallest / len(cuts), high / len(cuts))
        gain = gain * jnp.repeat(jnp.exp(heights), extent[axis_at] // shards_of).reshape((-1,) + (1,) * (len(extent) - 1 - axis_at))
    return gain


def normal_values(key, extent, deviation, reach, pieces=(), held_as=jnp.bfloat16):
    array = deviation * jax.random.normal(key, extent, jnp.float32)
    if pieces:
        array = array * level_of(key, extent, pieces, -0.22, 0.18)
    return jnp.clip(array, -reach, reach).astype(held_as)


def setup_inputs(seed: int = 0, part: int = 0) -> dict:
    key_of = jax.random.split(jax.random.key(seed), 7)
    own_keys = jax.random.split(jax.random.fold_in(key_of[6], part), 7)
    projected = normal_values(own_keys[0], (3, LENGTH, D), 1.0, 6.0, ((1, 16),))
    short_taps = normal_values(key_of[1], (SHORT, 3, D), 0.6, 3.0, (), jnp.float32)
    skip_gain = normal_values(key_of[2], (D,), 1.0, 3.0, (), jnp.float32)
    residues = normal_values(key_of[3], (2, STATE, D), LENGTH ** -0.5, 0.125, (), jnp.float32)
    pole_angles = jnp.clip(jax.random.uniform(key_of[4], (STATE, D), jnp.float32, -3.140625, 3.140625), -3.140625, 3.140625)
    decay_rates = draw_decay_rates(jax.random.fold_in(key_of[6], 71), part)
    return {"projected": projected, "short_taps": short_taps, "skip_gain": skip_gain, "residues": residues, "pole_angles": pole_angles, "decay_rates": decay_rates}


def filter_values(positions, residues, pole_angles, decay_rates):
    total = jnp.zeros((positions.shape[0], residues.shape[2]), jnp.float32)
    for state in range(residues.shape[1]):
        phase = pole_angles[state][None, :] * positions[:, None]
        damping = jnp.exp(-decay_rates[state][None, :] * positions[:, None])
        total = total + damping * (residues[0, state][None, :] * jnp.cos(phase) - residues[1, state][None, :] * jnp.sin(phase))
    return total.astype(jnp.bfloat16)


def reference(projected, short_taps, skip_gain, residues, pole_angles, decay_rates):
    positions = jnp.arange(LENGTH).astype(jnp.float32)
    kernel = filter_values(positions, residues, pole_angles, decay_rates)
    padded = jnp.pad(projected.astype(jnp.float32), ((0, 0), (2, 0), (0, 0)))
    conv = (short_taps[0][:, None, :] * padded[:, 0:LENGTH]
            + short_taps[1][:, None, :] * padded[:, 1:LENGTH + 1]
            + short_taps[2][:, None, :] * padded[:, 2:LENGTH + 2])
    products = (conv[1] * conv[2]).astype(jnp.bfloat16)
    doubled = 2 * LENGTH
    spectrum = jnp.fft.rfft(products.astype(jnp.float32), n=doubled, axis=0) * jnp.fft.rfft(kernel.astype(jnp.float32), n=doubled, axis=0)
    long_sum = jnp.fft.irfft(spectrum, n=doubled, axis=0)[:LENGTH]
    long_rounded = lax.optimization_barrier(long_sum.astype(jnp.bfloat16))
    gated = conv[0] * (long_rounded.astype(jnp.float32) + skip_gain[None, :] * products.astype(jnp.float32))
    return gated.astype(jnp.bfloat16)
```

```python
import functools

import jax
import jax.numpy as jnp
from jax import lax
from jax.experimental import pallas as pl
from jax.experimental.pallas import tpu as pltpu
from jax.sharding import PartitionSpec as P

MESH = pl.DeviceIdType.MESH
LANES = 128
CHUNKS = 8
WIDE = 256
F32 = jnp.float32
BF16 = jnp.bfloat16

RE1, IM1, C1, C2, RE16, IM16, RE32, IM32, RE64, IM64, RE128, IM128, G0, G1, H1, H0R, H0I = range(17)
TABLE_ROWS = 17


def square(re, im):
    return re * re - im * im, 2.0 * (re * im)


def cos_sin_half(angle):
    x = 0.5 * angle
    z = x * x
    s = 1.0 / 6227020800.0
    for coefficient in (-1.0 / 39916800.0, 1.0 / 362880.0, -1.0 / 5040.0, 1.0 / 120.0, -1.0 / 6.0, 1.0):
        s = s * z + coefficient
    c = -1.0 / 87178291200.0
    for coefficient in (1.0 / 479001600.0, -1.0 / 3628800.0, 1.0 / 40320.0, -1.0 / 720.0, 1.0 / 24.0, -0.5, 1.0):
        c = c * z + coefficient
    return c, s * x


def kernel(
    n, owners, per_owner,
    x_hbm, taps_hbm, skip_hbm, res_hbm, ang_hbm, dec_hbm, out_hbm,
    xs, tail, taps, skip, res, ang, dec, to_chunks, to_rows, tab,
    halo_f32, halo_send, halo_recv, halo,
    prod, local, query, scan, t_send, t_in, c_out, c_in, rot_a, rot_b, outs,
    in_sems, kv_sems, out_sems, halo_sems, t_ssem, t_rsem, c_ssem, c_rsem,
):
    rows, width = xs.shape[1], xs.shape[2]
    steps = rows // CHUNKS
    half_width = width // 2
    blocks = width // WIDE
    kv_parts = kv_sems.shape[0]
    part_width = width // kv_parts
    msg_rows = t_send.shape[1]
    half_msg = msg_rows // 2
    me = lax.axis_index("seq")

    barrier = pltpu.get_barrier_semaphore()

    def greet(d, carry):
        pl.semaphore_signal(
            barrier, inc=1, device_id={"seq": lax.rem(me + d, n)}, device_id_type=MESH
        )
        return carry

    def kv_copy(part):
        cols = pl.ds(pl.multiple_of(part * part_width, part_width), part_width)
        return pltpu.make_async_copy(
            x_hbm.at[pl.ds(1, 2), :, cols], xs.at[pl.ds(1, 2), :, cols], kv_sems.at[part]
        )

    tail_copy = pltpu.make_async_copy(
        x_hbm.at[:, pl.ds(rows - 16, 16), :], tail, in_sems.at[0]
    )
    tail_copy.start()
    small = [
        pltpu.make_async_copy(source, target, in_sems.at[1 + i])
        for i, (source, target) in enumerate(
            [(ang_hbm, ang), (dec_hbm, dec), (res_hbm, res), (taps_hbm, taps), (skip_hbm, skip)]
        )
    ]
    for copy in small:
        copy.start()
    for part in range(kv_parts):
        kv_copy(part).start()
    q_copy = pltpu.make_async_copy(x_hbm.at[0], xs.at[0], in_sems.at[6])
    q_copy.start()
    lax.fori_loop(1, n, greet, 0)

    i0 = lax.broadcasted_iota(jnp.int32, (rows, rows), 0)
    i1 = lax.broadcasted_iota(jnp.int32, (rows, rows), 1)
    to_chunks[...] = jnp.where(i1 == (i0 % CHUNKS) * steps + i0 // CHUNKS, 1.0, 0.0).astype(BF16)
    to_rows[...] = jnp.where(i0 == (i1 % CHUNKS) * steps + i1 // CHUNKS, 1.0, 0.0).astype(BF16)

    tail_copy.wait()
    for i in range(3):
        last = tail[i].astype(F32)[14:16]
        halo_f32[2 * i : 2 * i + 2, :] = last[:, :half_width]
        halo_f32[8 + 2 * i : 10 + 2 * i, :] = last[:, half_width:]
    halo_f32[6:8, :] = jnp.zeros((2, half_width), F32)
    halo_f32[14:16, :] = jnp.zeros((2, half_width), F32)
    halo_send[...] = halo_f32[...].astype(BF16)
    halo_copy = pltpu.make_async_remote_copy(
        src_ref=halo_send,
        dst_ref=halo_recv,
        send_sem=halo_sems.at[0],
        recv_sem=halo_sems.at[1],
        device_id={"seq": lax.rem(me + 1, n)},
        device_id_type=MESH,
    )
    pl.semaphore_wait(barrier, n - 1)
    pl.when(me < n - 1)(halo_copy.start)

    for copy in small:
        copy.wait()

    def parameters(b, carry):
        cols = pl.ds(pl.multiple_of(b * WIDE, WIDE), WIDE)
        c, s = cos_sin_half(ang[:, cols])
        root = jnp.exp(-0.5 * dec[:, cols])
        re, im = square(root * c, root * s)
        r0, r1 = res[0, :, cols], res[1, :, cols]
        tab[RE1, :, cols] = re
        tab[IM1, :, cols] = im
        tab[C1, :, cols] = 2.0 * re
        tab[C2, :, cols] = -(re * re + im * im)
        tab[G0, :, cols] = r0
        tab[G1, :, cols] = -(r0 * re + r1 * im)
        tab[H1, :, cols] = -r1
        tab[H0R, :, cols] = r0 * re - r1 * im
        tab[H0I, :, cols] = -(r0 * im + r1 * re)
        power = 1
        while power < rows:
            re, im = square(re, im)
            power *= 2
            if power == steps:
                tab[RE16, :, cols], tab[IM16, :, cols] = re, im
            elif power == 2 * steps:
                tab[RE32, :, cols], tab[IM32, :, cols] = re, im
            elif power == 4 * steps:
                tab[RE64, :, cols], tab[IM64, :, cols] = re, im
            elif power == 8 * steps:
                tab[RE128, :, cols], tab[IM128, :, cols] = re, im
        return carry

    lax.fori_loop(0, blocks, parameters, 0)
    if 4 * per_owner < msg_rows:
        t_send[...] = jnp.zeros(t_send.shape, F32)
        rot_a[...] = jnp.zeros(rot_a.shape, F32)
        rot_b[...] = jnp.zeros(rot_b.shape, F32)
    own = lax.rem(me, owners)
    for pole in range(2):
        for k in range(per_owner):
            cols = pl.ds(pl.multiple_of((own * per_owner + k) * LANES, LANES), LANES)
            re, im = tab[RE128, pole : pole + 1, cols], tab[IM128, pole : pole + 1, cols]
            row = pole * per_owner + k
            rot_a[row : row + 1, :] = re
            rot_a[half_msg + row : half_msg + row + 1, :] = re
            rot_b[row : row + 1, :] = -im
            rot_b[half_msg + row : half_msg + row + 1, :] = im

    pl.when(me > 0)(halo_copy.wait_recv)
    keep = me > 0
    received = halo_recv[...].astype(F32)
    received = jnp.where(keep, received, jnp.zeros_like(received))
    halo[:, 0:half_width] = received[0:8]
    halo[:, half_width:width] = received[8:16]

    sub = lax.broadcasted_iota(jnp.int32, (CHUNKS, WIDE), 0)
    first = sub == 0

    def param(which, pole, cols):
        return tab[which, pole : pole + 1, cols]

    def short(i, cols):
        x = jnp.dot(to_chunks[...], xs[i, :, cols], preferred_element_type=F32)
        at = [x[CHUNKS * r : CHUNKS * (r + 1)] for r in range(steps)]
        before2 = jnp.where(first, halo[2 * i : 2 * i + 1, cols], pltpu.roll(at[steps - 2], 1, 0))
        before1 = jnp.where(first, halo[2 * i + 1 : 2 * i + 2, cols], pltpu.roll(at[steps - 1], 1, 0))
        at = [before2, before1] + at
        w = [taps[tap, i : i + 1, cols] for tap in range(3)]
        return [w[0] * at[r] + w[1] * at[r + 1] + w[2] * at[r + 2] for r in range(steps)]

    def message_place(b, k):
        if per_owner == 1:
            return (WIDE // LANES) * b + k, 0
        tile = (WIDE // LANES) * b + k
        return tile // per_owner, tile % per_owner

    def pass_a(b, carry):
        cols = pl.ds(pl.multiple_of(b * WIDE, WIDE), WIDE)
        key = short(1, cols)
        value = short(2, cols)
        c1 = [param(C1, pole, cols) for pole in range(2)]
        c2 = [param(C2, pole, cols) for pole in range(2)]
        now = [jnp.zeros((CHUNKS, WIDE), F32)] * 2
        old = [jnp.zeros((CHUNKS, WIDE), F32)] * 2
        for r in range(steps):
            p = key[r] * value[r]
            prod[CHUNKS * r : CHUNKS * (r + 1), cols] = p
            for pole in range(2):
                now[pole], old[pole] = p + c1[pole] * now[pole] + c2[pole] * old[pole], now[pole]
        for pole in range(2):
            re = now[pole] - param(RE1, pole, cols) * old[pole]
            im = param(IM1, pole, cols) * old[pole]
            for shift, wr, wi in ((1, RE16, IM16), (2, RE32, IM32), (4, RE64, IM64)):
                wr, wi = param(wr, pole, cols), param(wi, pole, cols)
                far = sub >= shift
                pr = jnp.where(far, pltpu.roll(re, shift, 0), 0.0)
                pi = jnp.where(far, pltpu.roll(im, shift, 0), 0.0)
                re, im = re + (wr * pr - wi * pi), im + (wr * pi + wi * pr)
            scan[2 * pole, :, cols] = jnp.where(first, 0.0, pltpu.roll(re, 1, 0))
            scan[2 * pole + 1, :, cols] = jnp.where(first, 0.0, pltpu.roll(im, 1, 0))
            for k in range(WIDE // LANES):
                owner, kk = message_place(b, k)
                lanes = slice(k * LANES, (k + 1) * LANES)
                row = pole * per_owner + kk
                t_send[owner, pl.ds(row, 1), :] = re[CHUNKS - 1 : CHUNKS, lanes]
                t_send[owner, pl.ds(half_msg + row, 1), :] = im[CHUNKS - 1 : CHUNKS, lanes]
        return carry

    def part_a(part, carry):
        kv_copy(part).wait()
        each = part_width // WIDE
        return lax.fori_loop(part * each, (part + 1) * each, pass_a, carry)

    lax.fori_loop(0, kv_parts, part_a, 0)

    def t_copy(source, target):
        return pltpu.make_async_remote_copy(
            src_ref=t_send.at[target],
            dst_ref=t_in.at[source],
            send_sem=t_ssem.at[target],
            recv_sem=t_rsem.at[source],
            device_id={"seq": target},
            device_id_type=MESH,
        )

    def c_copy(source, target):
        return pltpu.make_async_remote_copy(
            src_ref=c_out.at[target],
            dst_ref=c_in.at[source],
            send_sem=c_ssem.at[target],
            recv_sem=c_rsem.at[source],
            device_id={"seq": target},
            device_id_type=MESH,
        )

    def when_owner(device, action):
        if owners == n:
            action()
        else:
            pl.when(device < owners)(action)

    def send_t(d, carry):
        target = lax.rem(me + d, n)
        when_owner(target, lambda: t_copy(me, target).start())
        return carry

    lax.fori_loop(1, n, send_t, 0)

    q_copy.wait()

    def pass_b(b, carry):
        cols = pl.ds(pl.multiple_of(b * WIDE, WIDE), WIDE)
        for r, values in enumerate(short(0, cols)):
            query[CHUNKS * r : CHUNKS * (r + 1), cols] = values
        return carry

    def pass_b2(b, carry):
        cols = pl.ds(pl.multiple_of(b * WIDE, WIDE), WIDE)
        c1 = [param(C1, pole, cols) for pole in range(2)]
        c2 = [param(C2, pole, cols) for pole in range(2)]
        g0 = [param(G0, pole, cols) for pole in range(2)]
        g1 = [param(G1, pole, cols) for pole in range(2)]
        gain = skip[:, cols]
        zero = jnp.zeros((CHUNKS, WIDE), F32)
        now, old, before = [zero] * 2, [zero] * 2, zero
        for r in range(steps):
            p = prod[CHUNKS * r : CHUNKS * (r + 1), cols]
            for pole in range(2):
                fresh = g0[pole] * p + g1[pole] * before + c1[pole] * now[pole] + c2[pole] * old[pole]
                now[pole], old[pole] = fresh, now[pole]
            local[CHUNKS * r : CHUNKS * (r + 1), cols] = now[0] + now[1] + gain * p
            before = p
        return carry

    lax.fori_loop(0, blocks, pass_b, 0)

    def owner_step():
        t_in[pl.ds(me, 1)] = t_send[pl.ds(own, 1)]

        def wait_t(d, carry):
            t_copy(lax.rem(me + d, n), me).wait_recv()
            return carry

        lax.fori_loop(1, n, wait_t, 0)
        a, bb = rot_a[...], rot_b[...]

        def prefix(i, state):
            c_out[i] = state
            return a * state + bb * pltpu.roll(state, half_msg, 0) + t_in[i]

        lax.fori_loop(0, n, prefix, jnp.zeros((msg_rows, LANES), F32))

        def send_c(d, carry):
            c_copy(me, lax.rem(me + d, n)).start()
            return carry

        lax.fori_loop(1, n, send_c, 0)
        c_in[pl.ds(own, 1)] = c_out[pl.ds(me, 1)]

    when_owner(me, owner_step)

    lax.fori_loop(0, blocks, pass_b2, 0)

    def wait_c(d, carry):
        source = lax.rem(me + d, n)
        when_owner(source, lambda: c_copy(source, me).wait_recv())
        return carry

    lax.fori_loop(1, n, wait_c, 0)

    def out_copy(b):
        cols = pl.ds(pl.multiple_of(b * WIDE, WIDE), WIDE)
        return pltpu.make_async_copy(outs.at[:, cols], out_hbm.at[:, cols], out_sems.at[b])

    def pass_c(b, carry):
        cols = pl.ds(pl.multiple_of(b * WIDE, WIDE), WIDE)
        c1 = [param(C1, pole, cols) for pole in range(2)]
        c2 = [param(C2, pole, cols) for pole in range(2)]
        now, old = [], []
        for pole in range(2):
            cr, ci = [], []
            for k in range(WIDE // LANES):
                owner, kk = message_place(b, k)
                row = pole * per_owner + kk
                cr.append(c_in[owner, pl.ds(row, 1), :])
                ci.append(c_in[owner, pl.ds(half_msg + row, 1), :])
            cr = jnp.broadcast_to(jnp.concatenate(cr, axis=1), (CHUNKS, WIDE))
            ci = jnp.broadcast_to(jnp.concatenate(ci, axis=1), (CHUNKS, WIDE))
            for bit, wr, wi in ((1, RE16, IM16), (2, RE32, IM32), (4, RE64, IM64)):
                wr, wi = param(wr, pole, cols), param(wi, pole, cols)
                has = (sub // bit) % 2 == 1
                cr, ci = (
                    jnp.where(has, wr * cr - wi * ci, cr),
                    jnp.where(has, wr * ci + wi * cr, ci),
                )
            zr = scan[2 * pole, :, cols] + cr
            zi = scan[2 * pole + 1, :, cols] + ci
            old.append(param(G0, pole, cols) * zr + param(H1, pole, cols) * zi)
            now.append(param(H0R, pole, cols) * zr + param(H0I, pole, cols) * zi)
        done = []
        for r in range(steps):
            at = slice(CHUNKS * r, CHUNKS * (r + 1))
            done.append(query[at, cols] * (local[at, cols] + (now[0] + now[1])))
            for pole in range(2):
                now[pole], old[pole] = c1[pole] * now[pole] + c2[pole] * old[pole], now[pole]
        gated = jnp.concatenate(done, axis=0).astype(BF16)
        outs[:, cols] = jnp.dot(to_rows[...], gated, preferred_element_type=F32).astype(BF16)
        out_copy(b).start()
        return carry

    lax.fori_loop(0, blocks, pass_c, 0)

    def wait_out(b, carry):
        out_copy(b).wait()
        return carry

    lax.fori_loop(0, blocks, wait_out, 0)

    def drain(d, carry):
        target = lax.rem(me + d, n)
        when_owner(target, lambda: t_copy(me, target).wait_send())
        when_owner(me, lambda: c_copy(me, target).wait_send())
        return carry

    lax.fori_loop(1, n, drain, 0)
    pl.when(me < n - 1)(halo_copy.wait_send)


def solution(mesh):
    n = mesh.shape["seq"]

    def on_device(projected, short_taps, skip_gain, residues, pole_angles, decay_rates):
        _, rows, width = projected.shape
        tiles = width // LANES
        owners = min(n, tiles)
        per_owner = tiles // owners
        msg_rows = max(8, 4 * per_owner)
        kv_parts = 4
        dma = pltpu.SemaphoreType.DMA
        vmem = pltpu.VMEM
        return pl.pallas_call(
            functools.partial(kernel, n, owners, per_owner),
            out_shape=jax.ShapeDtypeStruct((rows, width), BF16),
            in_specs=[pl.BlockSpec(memory_space=pl.ANY)] * 6,
            out_specs=pl.BlockSpec(memory_space=pl.ANY),
            scratch_shapes=[
                vmem((3, rows, width), BF16),
                vmem((3, 16, width), BF16),
                vmem(short_taps.shape, F32),
                vmem((1, width), F32),
                vmem(residues.shape, F32),
                vmem(pole_angles.shape, F32),
                vmem(decay_rates.shape, F32),
                vmem((rows, rows), BF16),
                vmem((rows, rows), BF16),
                vmem((TABLE_ROWS, 2, width), F32),
                vmem((16, width // 2), F32),
                vmem((16, width // 2), BF16),
                vmem((16, width // 2), BF16),
                vmem((8, width), F32),
                vmem((rows, width), F32),
                vmem((rows, width), F32),
                vmem((rows, width), F32),
                vmem((4, CHUNKS, width), F32),
                vmem((owners, msg_rows, LANES), F32),
                vmem((n, msg_rows, LANES), F32),
                vmem((n, msg_rows, LANES), F32),
                vmem((owners, msg_rows, LANES), F32),
                vmem((msg_rows, LANES), F32),
                vmem((msg_rows, LANES), F32),
                vmem((rows, width), BF16),
                dma((7,)),
                dma((kv_parts,)),
                dma((width // WIDE,)),
                dma((2,)),
                dma((n,)),
                dma((n,)),
                dma((n,)),
                dma((n,)),
            ],
            compiler_params=pltpu.CompilerParams(
                collective_id=0, has_side_effects=True, vmem_limit_bytes=40 * 1024 * 1024
            ),
            cost_estimate=pl.CostEstimate(
                flops=60 * rows * width, bytes_accessed=8 * rows * width, transcendentals=2 * width
            ),
        )(projected, short_taps, skip_gain.reshape(1, width), residues, pole_angles, decay_rates)

    return jax.shard_map(
        on_device,
        mesh=mesh,
        in_specs=(P(None, ("grp", "seq"), None), P(), P(), P(), P(), P()),
        out_specs=P(("grp", "seq"), None),
        check_vma=False,
    )
```

```python
import functools

import jax
import jax.numpy as jnp
from jax import lax
from jax.experimental import pallas as pl
from jax.experimental.pallas import tpu as pltpu
from jax.sharding import PartitionSpec as P

MESH = pl.DeviceIdType.MESH
LANES = 128
CHUNKS = 8
WIDE = 512
F32 = jnp.float32
BF16 = jnp.bfloat16

RE1, IM1, C1, C2, RE16, IM16, RE32, IM32, RE64, IM64, RE128, IM128, G0, G1, H1, H0R, H0I = range(17)
TABLE_ROWS = 17


def square(re, im):
    return re * re - im * im, 2.0 * (re * im)


def cos_sin_half(angle):
    x = 0.5 * angle
    z = x * x
    s = 1.0 / 6227020800.0
    for coefficient in (-1.0 / 39916800.0, 1.0 / 362880.0, -1.0 / 5040.0, 1.0 / 120.0, -1.0 / 6.0, 1.0):
        s = s * z + coefficient
    c = -1.0 / 87178291200.0
    for coefficient in (1.0 / 479001600.0, -1.0 / 3628800.0, 1.0 / 40320.0, -1.0 / 720.0, 1.0 / 24.0, -0.5, 1.0):
        c = c * z + coefficient
    return c, s * x


def kernel(
    n, owners, per_owner,
    x_hbm, taps_hbm, skip_hbm, res_hbm, ang_hbm, dec_hbm, out_hbm,
    xs, ordered, tail, taps, skip, res, ang, dec, to_chunks, to_rows, tab,
    halo_f32, halo_send, halo_recv, halo,
    prod, local, query, scan, t_send, t_in, c_out, c_in, rot_a, rot_b, outs,
    in_sems, kv_sems, out_sems, halo_sems, t_ssem, t_rsem, c_ssem, c_rsem,
):
    rows, width = xs.shape[1], xs.shape[2]
    steps = rows // CHUNKS
    half_width = width // 2
    blocks = width // WIDE
    kv_parts = kv_sems.shape[0]
    part_width = width // kv_parts
    msg_rows = t_send.shape[1]
    half_msg = msg_rows // 2
    me = lax.axis_index("seq")

    barrier = pltpu.get_barrier_semaphore()

    def greet(d, carry):
        pl.semaphore_signal(
            barrier, inc=1, device_id={"seq": lax.rem(me + d, n)}, device_id_type=MESH
        )
        return carry

    def kv_copy(part):
        cols = pl.ds(pl.multiple_of(part * part_width, part_width), part_width)
        return pltpu.make_async_copy(
            x_hbm.at[pl.ds(1, 2), :, cols], xs.at[pl.ds(1, 2), :, cols], kv_sems.at[part]
        )

    tail_copy = pltpu.make_async_copy(
        x_hbm.at[:, pl.ds(rows - 16, 16), :], tail, in_sems.at[0]
    )
    tail_copy.start()
    small = [
        pltpu.make_async_copy(source, target, in_sems.at[1 + i])
        for i, (source, target) in enumerate(
            [(ang_hbm, ang), (dec_hbm, dec), (res_hbm, res), (taps_hbm, taps), (skip_hbm, skip)]
        )
    ]
    for copy in small:
        copy.start()
    for part in range(kv_parts):
        kv_copy(part).start()
    q_copy = pltpu.make_async_copy(x_hbm.at[0], xs.at[0], in_sems.at[6])
    q_copy.start()
    lax.fori_loop(1, n, greet, 0)

    i0 = lax.broadcasted_iota(jnp.int32, (rows, rows), 0)
    i1 = lax.broadcasted_iota(jnp.int32, (rows, rows), 1)
    to_chunks[...] = jnp.where(i1 == (i0 % CHUNKS) * steps + i0 // CHUNKS, 1.0, 0.0).astype(BF16)
    to_rows[...] = jnp.where(i0 == (i1 % CHUNKS) * steps + i1 // CHUNKS, 1.0, 0.0).astype(BF16)

    tail_copy.wait()
    for i in range(3):
        last = tail[i].astype(F32)[14:16]
        halo_f32[2 * i : 2 * i + 2, :] = last[:, :half_width]
        halo_f32[8 + 2 * i : 10 + 2 * i, :] = last[:, half_width:]
    halo_f32[6:8, :] = jnp.zeros((2, half_width), F32)
    halo_f32[14:16, :] = jnp.zeros((2, half_width), F32)
    halo_send[...] = halo_f32[...].astype(BF16)
    halo_copy = pltpu.make_async_remote_copy(
        src_ref=halo_send,
        dst_ref=halo_recv,
        send_sem=halo_sems.at[0],
        recv_sem=halo_sems.at[1],
        device_id={"seq": lax.rem(me + 1, n)},
        device_id_type=MESH,
    )
    for copy in small:
        copy.wait()

    def parameters(b, carry):
        cols = pl.ds(pl.multiple_of(b * part_width, part_width), part_width)
        c, s = cos_sin_half(ang[:, cols])
        root = jnp.exp(-0.5 * dec[:, cols])
        re, im = square(root * c, root * s)
        r0, r1 = res[0, :, cols], res[1, :, cols]
        tab[RE1, :, cols] = re
        tab[IM1, :, cols] = im
        tab[C1, :, cols] = 2.0 * re
        tab[C2, :, cols] = -(re * re + im * im)
        tab[G0, :, cols] = r0
        tab[G1, :, cols] = -(r0 * re + r1 * im)
        tab[H1, :, cols] = -r1
        tab[H0R, :, cols] = r0 * re - r1 * im
        tab[H0I, :, cols] = -(r0 * im + r1 * re)
        power = 1
        while power < rows:
            re, im = square(re, im)
            power *= 2
            if power == steps:
                tab[RE16, :, cols], tab[IM16, :, cols] = re, im
            elif power == 2 * steps:
                tab[RE32, :, cols], tab[IM32, :, cols] = re, im
            elif power == 4 * steps:
                tab[RE64, :, cols], tab[IM64, :, cols] = re, im
            elif power == 8 * steps:
                tab[RE128, :, cols], tab[IM128, :, cols] = re, im
        return carry

    lax.fori_loop(0, kv_parts, parameters, 0)
    pl.semaphore_wait(barrier, n - 1)
    pl.when(me < n - 1)(halo_copy.start)

    def order(i, part):
        cols = pl.ds(pl.multiple_of(part * part_width, part_width), part_width)
        ordered[i, :, cols] = jnp.dot(to_chunks[...], xs[i, :, cols], preferred_element_type=F32)

    def order_kv(part, carry):
        kv_copy(part).wait()
        order(1, part)
        order(2, part)
        return carry

    lax.fori_loop(0, kv_parts, order_kv, 0)

    if 4 * per_owner < msg_rows:
        t_send[...] = jnp.zeros(t_send.shape, F32)
        rot_a[...] = jnp.zeros(rot_a.shape, F32)
        rot_b[...] = jnp.zeros(rot_b.shape, F32)
    own = lax.rem(me, owners)
    for pole in range(2):
        for k in range(per_owner):
            cols = pl.ds(pl.multiple_of((own * per_owner + k) * LANES, LANES), LANES)
            re, im = tab[RE128, pole : pole + 1, cols], tab[IM128, pole : pole + 1, cols]
            row = pole * per_owner + k
            rot_a[row : row + 1, :] = re
            rot_a[half_msg + row : half_msg + row + 1, :] = re
            rot_b[row : row + 1, :] = -im
            rot_b[half_msg + row : half_msg + row + 1, :] = im

    pl.when(me > 0)(halo_copy.wait_recv)
    keep = me > 0
    received = halo_recv[...].astype(F32)
    received = jnp.where(keep, received, jnp.zeros_like(received))
    halo[:, 0:half_width] = received[0:8]
    halo[:, half_width:width] = received[8:16]

    sub = lax.broadcasted_iota(jnp.int32, (CHUNKS, WIDE), 0)
    first = sub == 0

    def param(which, pole, cols):
        return tab[which, pole : pole + 1, cols]

    def short(i, cols):
        at = [ordered[i, CHUNKS * r : CHUNKS * (r + 1), cols] for r in range(steps)]
        before2 = jnp.where(first, halo[2 * i : 2 * i + 1, cols], pltpu.roll(at[steps - 2], 1, 0))
        before1 = jnp.where(first, halo[2 * i + 1 : 2 * i + 2, cols], pltpu.roll(at[steps - 1], 1, 0))
        at = [before2, before1] + at
        w = [taps[tap, i : i + 1, cols] for tap in range(3)]
        return [w[0] * at[r] + w[1] * at[r + 1] + w[2] * at[r + 2] for r in range(steps)]

    def message_place(b, k):
        if per_owner == 1:
            return (WIDE // LANES) * b + k, 0
        tile = (WIDE // LANES) * b + k
        return tile // per_owner, tile % per_owner

    def pass_a(b, carry):
        cols = pl.ds(pl.multiple_of(b * WIDE, WIDE), WIDE)
        key = short(1, cols)
        value = short(2, cols)
        c1 = [param(C1, pole, cols) for pole in range(2)]
        c2 = [param(C2, pole, cols) for pole in range(2)]
        now = [jnp.zeros((CHUNKS, WIDE), F32)] * 2
        old = [jnp.zeros((CHUNKS, WIDE), F32)] * 2
        for r in range(steps):
            p = key[r] * value[r]
            prod[CHUNKS * r : CHUNKS * (r + 1), cols] = p
            for pole in range(2):
                now[pole], old[pole] = p + c1[pole] * now[pole] + c2[pole] * old[pole], now[pole]
        for pole in range(2):
            re = now[pole] - param(RE1, pole, cols) * old[pole]
            im = param(IM1, pole, cols) * old[pole]
            for shift, wr, wi in ((1, RE16, IM16), (2, RE32, IM32), (4, RE64, IM64)):
                wr, wi = param(wr, pole, cols), param(wi, pole, cols)
                far = sub >= shift
                pr = jnp.where(far, pltpu.roll(re, shift, 0), 0.0)
                pi = jnp.where(far, pltpu.roll(im, shift, 0), 0.0)
                re, im = re + (wr * pr - wi * pi), im + (wr * pi + wi * pr)
            scan[2 * pole, :, cols] = jnp.where(first, 0.0, pltpu.roll(re, 1, 0))
            scan[2 * pole + 1, :, cols] = jnp.where(first, 0.0, pltpu.roll(im, 1, 0))
            for k in range(WIDE // LANES):
                owner, kk = message_place(b, k)
                lanes = slice(k * LANES, (k + 1) * LANES)
                row = pole * per_owner + kk
                t_send[owner, pl.ds(row, 1), :] = re[CHUNKS - 1 : CHUNKS, lanes]
                t_send[owner, pl.ds(half_msg + row, 1), :] = im[CHUNKS - 1 : CHUNKS, lanes]
        return carry

    lax.fori_loop(0, blocks, pass_a, 0)

    def t_copy(source, target):
        return pltpu.make_async_remote_copy(
            src_ref=t_send.at[target],
            dst_ref=t_in.at[source],
            send_sem=t_ssem.at[target],
            recv_sem=t_rsem.at[source],
            device_id={"seq": target},
            device_id_type=MESH,
        )

    def c_copy(source, target):
        return pltpu.make_async_remote_copy(
            src_ref=c_out.at[target],
            dst_ref=c_in.at[source],
            send_sem=c_ssem.at[target],
            recv_sem=c_rsem.at[source],
            device_id={"seq": target},
            device_id_type=MESH,
        )

    def when_owner(device, action):
        if owners == n:
            action()
        else:
            pl.when(device < owners)(action)

    def send_t(d, carry):
        target = lax.rem(me + d, n)
        when_owner(target, lambda: t_copy(me, target).start())
        return carry

    lax.fori_loop(1, n, send_t, 0)

    q_copy.wait()

    def order_q(part, carry):
        order(0, part)
        return carry

    lax.fori_loop(0, kv_parts, order_q, 0)

    def pass_b(b, carry):
        cols = pl.ds(pl.multiple_of(b * WIDE, WIDE), WIDE)
        for r, values in enumerate(short(0, cols)):
            query[CHUNKS * r : CHUNKS * (r + 1), cols] = values
        return carry

    def pass_b2(b, carry):
        cols = pl.ds(pl.multiple_of(b * WIDE, WIDE), WIDE)
        c1 = [param(C1, pole, cols) for pole in range(2)]
        c2 = [param(C2, pole, cols) for pole in range(2)]
        g0 = [param(G0, pole, cols) for pole in range(2)]
        g1 = [param(G1, pole, cols) for pole in range(2)]
        gain = skip[:, cols]
        zero = jnp.zeros((CHUNKS, WIDE), F32)
        now, old, before = [zero] * 2, [zero] * 2, zero
        for r in range(steps):
            p = prod[CHUNKS * r : CHUNKS * (r + 1), cols]
            for pole in range(2):
                fresh = g0[pole] * p + g1[pole] * before + c1[pole] * now[pole] + c2[pole] * old[pole]
                now[pole], old[pole] = fresh, now[pole]
            local[CHUNKS * r : CHUNKS * (r + 1), cols] = now[0] + now[1] + gain * p
            before = p
        return carry

    lax.fori_loop(0, blocks, pass_b, 0)

    def owner_step():
        t_in[pl.ds(me, 1)] = t_send[pl.ds(own, 1)]

        def wait_t(d, carry):
            t_copy(lax.rem(me + d, n), me).wait_recv()
            return carry

        lax.fori_loop(1, n, wait_t, 0)
        a, bb = rot_a[...], rot_b[...]

        def prefix(i, state):
            c_out[i] = state
            return a * state + bb * pltpu.roll(state, half_msg, 0) + t_in[i]

        lax.fori_loop(0, n, prefix, jnp.zeros((msg_rows, LANES), F32))

        def send_c(d, carry):
            c_copy(me, lax.rem(me + d, n)).start()
            return carry

        lax.fori_loop(1, n, send_c, 0)
        c_in[pl.ds(own, 1)] = c_out[pl.ds(me, 1)]

    when_owner(me, owner_step)

    lax.fori_loop(0, blocks, pass_b2, 0)

    def wait_c(d, carry):
        source = lax.rem(me + d, n)
        when_owner(source, lambda: c_copy(source, me).wait_recv())
        return carry

    lax.fori_loop(1, n, wait_c, 0)

    def out_copy(b):
        cols = pl.ds(pl.multiple_of(b * WIDE, WIDE), WIDE)
        return pltpu.make_async_copy(outs.at[:, cols], out_hbm.at[:, cols], out_sems.at[b])

    def pass_c(b, carry):
        cols = pl.ds(pl.multiple_of(b * WIDE, WIDE), WIDE)
        c1 = [param(C1, pole, cols) for pole in range(2)]
        c2 = [param(C2, pole, cols) for pole in range(2)]
        now, old = [], []
        for pole in range(2):
            cr, ci = [], []
            for k in range(WIDE // LANES):
                owner, kk = message_place(b, k)
                row = pole * per_owner + kk
                cr.append(c_in[owner, pl.ds(row, 1), :])
                ci.append(c_in[owner, pl.ds(half_msg + row, 1), :])
            cr = jnp.broadcast_to(jnp.concatenate(cr, axis=1), (CHUNKS, WIDE))
            ci = jnp.broadcast_to(jnp.concatenate(ci, axis=1), (CHUNKS, WIDE))
            for bit, wr, wi in ((1, RE16, IM16), (2, RE32, IM32), (4, RE64, IM64)):
                wr, wi = param(wr, pole, cols), param(wi, pole, cols)
                has = (sub // bit) % 2 == 1
                cr, ci = (
                    jnp.where(has, wr * cr - wi * ci, cr),
                    jnp.where(has, wr * ci + wi * cr, ci),
                )
            zr = scan[2 * pole, :, cols] + cr
            zi = scan[2 * pole + 1, :, cols] + ci
            old.append(param(G0, pole, cols) * zr + param(H1, pole, cols) * zi)
            now.append(param(H0R, pole, cols) * zr + param(H0I, pole, cols) * zi)
        done = []
        for r in range(steps):
            at = slice(CHUNKS * r, CHUNKS * (r + 1))
            done.append(query[at, cols] * (local[at, cols] + (now[0] + now[1])))
            for pole in range(2):
                now[pole], old[pole] = c1[pole] * now[pole] + c2[pole] * old[pole], now[pole]
        gated = jnp.concatenate(done, axis=0).astype(BF16)
        outs[:, cols] = jnp.dot(to_rows[...], gated, preferred_element_type=F32).astype(BF16)
        out_copy(b).start()
        return carry

    lax.fori_loop(0, blocks, pass_c, 0)

    def wait_out(b, carry):
        out_copy(b).wait()
        return carry

    lax.fori_loop(0, blocks, wait_out, 0)

    def drain(d, carry):
        target = lax.rem(me + d, n)
        when_owner(target, lambda: t_copy(me, target).wait_send())
        when_owner(me, lambda: c_copy(me, target).wait_send())
        return carry

    lax.fori_loop(1, n, drain, 0)
    pl.when(me < n - 1)(halo_copy.wait_send)


def solution(mesh):
    n = mesh.shape["seq"]

    def on_device(projected, short_taps, skip_gain, residues, pole_angles, decay_rates):
        _, rows, width = projected.shape
        tiles = width // LANES
        owners = min(n, tiles)
        per_owner = tiles // owners
        msg_rows = max(8, 4 * per_owner)
        kv_parts = 4
        dma = pltpu.SemaphoreType.DMA
        vmem = pltpu.VMEM
        return pl.pallas_call(
            functools.partial(kernel, n, owners, per_owner),
            out_shape=jax.ShapeDtypeStruct((rows, width), BF16),
            in_specs=[pl.BlockSpec(memory_space=pl.ANY)] * 6,
            out_specs=pl.BlockSpec(memory_space=pl.ANY),
            scratch_shapes=[
                vmem((3, rows, width), BF16),
                vmem((3, rows, width), F32),
                vmem((3, 16, width), BF16),
                vmem(short_taps.shape, F32),
                vmem((1, width), F32),
                vmem(residues.shape, F32),
                vmem(pole_angles.shape, F32),
                vmem(decay_rates.shape, F32),
                vmem((rows, rows), BF16),
                vmem((rows, rows), BF16),
                vmem((TABLE_ROWS, 2, width), F32),
                vmem((16, width // 2), F32),
                vmem((16, width // 2), BF16),
                vmem((16, width // 2), BF16),
                vmem((8, width), F32),
                vmem((rows, width), F32),
                vmem((rows, width), F32),
                vmem((rows, width), F32),
                vmem((4, CHUNKS, width), F32),
                vmem((owners, msg_rows, LANES), F32),
                vmem((n, msg_rows, LANES), F32),
                vmem((n, msg_rows, LANES), F32),
                vmem((owners, msg_rows, LANES), F32),
                vmem((msg_rows, LANES), F32),
                vmem((msg_rows, LANES), F32),
                vmem((rows, width), BF16),
                dma((7,)),
                dma((kv_parts,)),
                dma((width // WIDE,)),
                dma((2,)),
                dma((n,)),
                dma((n,)),
                dma((n,)),
                dma((n,)),
            ],
            compiler_params=pltpu.CompilerParams(
                collective_id=0, has_side_effects=True, vmem_limit_bytes=63 * 1024 * 1024
            ),
            cost_estimate=pl.CostEstimate(
                flops=60 * rows * width, bytes_accessed=8 * rows * width, transcendentals=2 * width
            ),
        )(projected, short_taps, skip_gain.reshape(1, width), residues, pole_angles, decay_rates)

    return jax.shard_map(
        on_device,
        mesh=mesh,
        in_specs=(P(None, ("grp", "seq"), None), P(), P(), P(), P(), P()),
        out_specs=P(("grp", "seq"), None),
        check_vma=False,
    )
```

```python
import functools
import math

import jax
import jax.numpy as jnp
from jax import lax
from jax.experimental import pallas as pl
from jax.experimental.pallas import tpu as pltpu
from jax.sharding import PartitionSpec as P

MESH = pl.DeviceIdType.MESH
CHUNKS = 8
WIDE = 256
F32 = jnp.float32
BF16 = jnp.bfloat16

RE1, IM1, C1, C2, RE16, IM16, RE32, IM32, RE64, IM64, RE128, IM128, G0, G1, H1, H0R, H0I = range(17)
TABLE_ROWS = 17


def square(re, im):
    return re * re - im * im, 2.0 * (re * im)


def cos_sin_half(angle):
    x = 0.5 * angle
    z = x * x
    s = 1.0 / 6227020800.0
    for coefficient in (-1.0 / 39916800.0, 1.0 / 362880.0, -1.0 / 5040.0, 1.0 / 120.0, -1.0 / 6.0, 1.0):
        s = s * z + coefficient
    c = -1.0 / 87178291200.0
    for coefficient in (1.0 / 479001600.0, -1.0 / 3628800.0, 1.0 / 40320.0, -1.0 / 720.0, 1.0 / 24.0, -0.5, 1.0):
        c = c * z + coefficient
    return c, s * x


def kernel(
    n, members,
    x_hbm, taps_hbm, skip_hbm, res_hbm, ang_hbm, dec_hbm, out_hbm,
    xs, ordered, tail, taps, skip, res, ang, dec, to_chunks, to_rows, tab,
    halo_f32, halo_send, halo_recv, halo,
    prod, local, query, scan, t_send, t_in, c_out, c_in, chain_out, chain_in, outs,
    in_sems, kv_sems, out_sems, halo_sems, t_ssem, t_rsem, c_ssem, c_rsem, chain_sems, ready,
):
    rows, width = xs.shape[1], xs.shape[2]
    steps = rows // CHUNKS
    half_width = width // 2
    blocks = width // WIDE
    kv_parts = kv_sems.shape[0]
    part_width = width // kv_parts
    quarter = width // members
    me = lax.axis_index("seq")
    place = lax.rem(me, members)
    base = me - place
    has_group_before = base > 0
    has_group_after = base + members < n
    is_first = place == 0
    is_last = place == members - 1

    def peer(step):
        other = place + step
        return jnp.where(other >= members, other - members, other)

    barrier = pltpu.get_barrier_semaphore()

    def signal(semaphore, device):
        pl.semaphore_signal(semaphore, inc=1, device_id={"seq": device}, device_id_type=MESH)

    for step in range(1, members):
        signal(barrier, base + peer(step))

    @pl.when(has_group_after)
    def _():
        signal(barrier, me + members)

    @pl.when(has_group_after & is_last)
    def _():
        signal(barrier, me + 1)

    def kv_copy(part):
        cols = pl.ds(pl.multiple_of(part * part_width, part_width), part_width)
        return pltpu.make_async_copy(
            x_hbm.at[pl.ds(1, 2), :, cols], xs.at[pl.ds(1, 2), :, cols], kv_sems.at[part]
        )

    tail_copy = pltpu.make_async_copy(
        x_hbm.at[:, pl.ds(rows - 16, 16), :], tail, in_sems.at[0]
    )
    tail_copy.start()
    small = [
        pltpu.make_async_copy(source, target, in_sems.at[1 + i])
        for i, (source, target) in enumerate(
            [(ang_hbm, ang), (dec_hbm, dec), (res_hbm, res), (taps_hbm, taps), (skip_hbm, skip)]
        )
    ]
    for copy in small:
        copy.start()
    for part in range(kv_parts):
        kv_copy(part).start()
    q_copy = pltpu.make_async_copy(x_hbm.at[0], xs.at[0], in_sems.at[6])
    q_copy.start()

    i0 = lax.broadcasted_iota(jnp.int32, (rows, rows), 0)
    i1 = lax.broadcasted_iota(jnp.int32, (rows, rows), 1)
    to_chunks[...] = jnp.where(i1 == (i0 & (CHUNKS - 1)) * steps + (i0 >> 3), 1.0, 0.0).astype(BF16)
    to_rows[...] = jnp.where(i0 == (i1 & (CHUNKS - 1)) * steps + (i1 >> 3), 1.0, 0.0).astype(BF16)

    tail_copy.wait()
    for i in range(3):
        last = tail[i].astype(F32)[14:16]
        halo_f32[2 * i : 2 * i + 2, :] = last[:, :half_width]
        halo_f32[8 + 2 * i : 10 + 2 * i, :] = last[:, half_width:]
    halo_f32[6:8, :] = jnp.zeros((2, half_width), F32)
    halo_f32[14:16, :] = jnp.zeros((2, half_width), F32)
    halo_send[...] = halo_f32[...].astype(BF16)
    halo_copy = pltpu.make_async_remote_copy(
        src_ref=halo_send,
        dst_ref=halo_recv,
        send_sem=halo_sems.at[0],
        recv_sem=halo_sems.at[1],
        device_id={"seq": jnp.where(me < n - 1, me + 1, 0)},
        device_id_type=MESH,
    )
    for copy in small:
        copy.wait()

    def parameters(b, carry):
        cols = pl.ds(pl.multiple_of(b * part_width, part_width), part_width)
        c, s = cos_sin_half(ang[:, cols])
        root = jnp.exp(-0.5 * dec[:, cols])
        re, im = square(root * c, root * s)
        r0, r1 = res[0, :, cols], res[1, :, cols]
        tab[RE1, :, cols] = re
        tab[IM1, :, cols] = im
        tab[C1, :, cols] = 2.0 * re
        tab[C2, :, cols] = -(re * re + im * im)
        tab[G0, :, cols] = r0
        tab[G1, :, cols] = -(r0 * re + r1 * im)
        tab[H1, :, cols] = -r1
        tab[H0R, :, cols] = r0 * re - r1 * im
        tab[H0I, :, cols] = -(r0 * im + r1 * re)
        power = 1
        while power < rows:
            re, im = square(re, im)
            power *= 2
            if power == steps:
                tab[RE16, :, cols], tab[IM16, :, cols] = re, im
            elif power == 2 * steps:
                tab[RE32, :, cols], tab[IM32, :, cols] = re, im
            elif power == 4 * steps:
                tab[RE64, :, cols], tab[IM64, :, cols] = re, im
            elif power == 8 * steps:
                tab[RE128, :, cols], tab[IM128, :, cols] = re, im
        return carry

    lax.fori_loop(0, kv_parts, parameters, 0)
    before = jnp.where(has_group_before, 1, 0)
    pl.semaphore_wait(barrier, members - 1 + before + jnp.where(is_first, before, 0))

    @pl.when(has_group_before)
    def _():
        signal(ready.at[0], me - members)

    @pl.when(has_group_before & is_first)
    def _():
        signal(ready.at[1], me - 1)

    @pl.when(has_group_after & is_last)
    def _():
        pl.semaphore_wait(ready.at[1], 1)

    pl.when(me < n - 1)(halo_copy.start)

    def order(i, part):
        cols = pl.ds(pl.multiple_of(part * part_width, part_width), part_width)
        ordered[i, :, cols] = jnp.dot(to_chunks[...], xs[i, :, cols], preferred_element_type=F32)

    def order_kv(part, carry):
        kv_copy(part).wait()
        order(1, part)
        order(2, part)
        return carry

    lax.fori_loop(0, kv_parts, order_kv, 0)

    pl.when(me > 0)(halo_copy.wait_recv)
    keep = me > 0
    received = halo_recv[...].astype(F32)
    received = jnp.where(keep, received, jnp.zeros_like(received))
    halo[:, 0:half_width] = received[0:8]
    halo[:, half_width:width] = received[8:16]

    sub = lax.broadcasted_iota(jnp.int32, (CHUNKS, WIDE), 0)
    first = sub == 0

    def param(which, pole, cols):
        return jnp.broadcast_to(tab[which, pole : pole + 1, cols], (CHUNKS, WIDE))

    def short(i, cols):
        at = [ordered[i, CHUNKS * r : CHUNKS * (r + 1), cols] for r in range(steps)]
        before2 = jnp.where(first, halo[2 * i : 2 * i + 1, cols], pltpu.roll(at[steps - 2], 1, 0))
        before1 = jnp.where(first, halo[2 * i + 1 : 2 * i + 2, cols], pltpu.roll(at[steps - 1], 1, 0))
        at = [before2, before1] + at
        w = [jnp.broadcast_to(taps[tap, i : i + 1, cols], (CHUNKS, WIDE)) for tap in range(3)]
        return [w[0] * at[r] + w[1] * at[r + 1] + w[2] * at[r + 2] for r in range(steps)]

    def message_place(b):
        each = quarter // WIDE
        owner = b // each
        return owner, pl.ds(pl.multiple_of((b - owner * each) * WIDE, WIDE), WIDE)

    def pass_a(b, carry):
        cols = pl.ds(pl.multiple_of(b * WIDE, WIDE), WIDE)
        key = short(1, cols)
        value = short(2, cols)
        c1 = [param(C1, pole, cols) for pole in range(2)]
        c2 = [param(C2, pole, cols) for pole in range(2)]
        now = [jnp.zeros((CHUNKS, WIDE), F32)] * 2
        old = [jnp.zeros((CHUNKS, WIDE), F32)] * 2
        for r in range(steps):
            p = key[r] * value[r]
            prod[CHUNKS * r : CHUNKS * (r + 1), cols] = p
            for pole in range(2):
                now[pole], old[pole] = (p + c2[pole] * old[pole]) + c1[pole] * now[pole], now[pole]
        for pole in range(2):
            re = now[pole] - param(RE1, pole, cols) * old[pole]
            im = param(IM1, pole, cols) * old[pole]
            for shift, wr, wi in ((1, RE16, IM16), (2, RE32, IM32), (4, RE64, IM64)):
                wr, wi = param(wr, pole, cols), param(wi, pole, cols)
                far = sub >= shift
                pr = jnp.where(far, pltpu.roll(re, shift, 0), 0.0)
                pi = jnp.where(far, pltpu.roll(im, shift, 0), 0.0)
                re, im = re + (wr * pr - wi * pi), im + (wr * pi + wi * pr)
            scan[2 * pole, :, cols] = jnp.where(first, 0.0, pltpu.roll(re, 1, 0))
            scan[2 * pole + 1, :, cols] = jnp.where(first, 0.0, pltpu.roll(im, 1, 0))
            owner, there = message_place(b)
            t_send[owner, 0, pl.ds(pole, 1), there] = re[CHUNKS - 1 : CHUNKS]
            t_send[owner, 1, pl.ds(pole, 1), there] = im[CHUNKS - 1 : CHUNKS]
        return carry

    lax.fori_loop(0, blocks, pass_a, 0, unroll=2)

    def t_copy(source, target):
        return pltpu.make_async_remote_copy(
            src_ref=t_send.at[target],
            dst_ref=t_in.at[source],
            send_sem=t_ssem.at[target],
            recv_sem=t_rsem.at[source],
            device_id={"seq": base + target},
            device_id_type=MESH,
        )

    def c_copy(source, target):
        return pltpu.make_async_remote_copy(
            src_ref=c_out.at[target],
            dst_ref=c_in.at[source],
            send_sem=c_ssem.at[target],
            recv_sem=c_rsem.at[source],
            device_id={"seq": base + target},
            device_id_type=MESH,
        )

    chain_copy = pltpu.make_async_remote_copy(
        src_ref=chain_out,
        dst_ref=chain_in,
        send_sem=chain_sems.at[0],
        recv_sem=chain_sems.at[1],
        device_id={"seq": jnp.where(has_group_after, me + members, me - base)},
        device_id_type=MESH,
    )
    for step in range(1, members):
        t_copy(place, peer(step)).start()

    q_copy.wait()

    def order_q(part, carry):
        order(0, part)
        return carry

    lax.fori_loop(0, kv_parts, order_q, 0)

    def pass_b(b, carry):
        cols = pl.ds(pl.multiple_of(b * WIDE, WIDE), WIDE)
        for r, values in enumerate(short(0, cols)):
            query[CHUNKS * r : CHUNKS * (r + 1), cols] = values
        return carry

    def pass_b2(b, carry):
        cols = pl.ds(pl.multiple_of(b * WIDE, WIDE), WIDE)
        c1 = [param(C1, pole, cols) for pole in range(2)]
        c2 = [param(C2, pole, cols) for pole in range(2)]
        g0 = [param(G0, pole, cols) for pole in range(2)]
        g1 = [param(G1, pole, cols) for pole in range(2)]
        gain = jnp.broadcast_to(skip[:, cols], (CHUNKS, WIDE))
        zero = jnp.zeros((CHUNKS, WIDE), F32)
        now, old, before = [zero] * 2, [zero] * 2, zero
        for r in range(steps):
            p = prod[CHUNKS * r : CHUNKS * (r + 1), cols]
            for pole in range(2):
                fresh = ((g0[pole] * p + g1[pole] * before) + c2[pole] * old[pole]) + c1[pole] * now[pole]
                now[pole], old[pole] = fresh, now[pole]
            local[CHUNKS * r : CHUNKS * (r + 1), cols] = now[0] + now[1] + gain * p
            before = p
        return carry

    lax.fori_loop(0, blocks, pass_b, 0, unroll=2)

    t_in[pl.ds(place, 1)] = t_send[pl.ds(place, 1)]
    for step in range(1, members):
        t_copy(peer(step), place).wait_recv()

    @pl.when(has_group_before)
    def _():
        chain_copy.wait_recv()

    @pl.when(jnp.logical_not(has_group_before))
    def _():
        chain_in[...] = jnp.zeros(chain_in.shape, F32)

    mine = pl.ds(pl.multiple_of(place * quarter, quarter), quarter)
    wr, wi = tab[RE128, :, mine], tab[IM128, :, mine]
    re, im = chain_in[0], chain_in[1]
    for member in range(members):
        c_out[member, 0] = re
        c_out[member, 1] = im
        re, im = (
            wr * re - wi * im + t_in[member, 0],
            wr * im + wi * re + t_in[member, 1],
        )
    chain_out[0] = re
    chain_out[1] = im

    @pl.when(has_group_after)
    def _():
        pl.semaphore_wait(ready.at[0], 1)
        chain_copy.start()

    for step in range(1, members):
        c_copy(place, peer(step)).start()
    c_in[pl.ds(place, 1)] = c_out[pl.ds(place, 1)]

    lax.fori_loop(0, blocks, pass_b2, 0, unroll=2)

    for step in range(1, members):
        c_copy(peer(step), place).wait_recv()

    def out_copy(b):
        cols = pl.ds(pl.multiple_of(b * WIDE, WIDE), WIDE)
        return pltpu.make_async_copy(outs.at[:, cols], out_hbm.at[:, cols], out_sems.at[b])

    def pass_c(b, carry):
        cols = pl.ds(pl.multiple_of(b * WIDE, WIDE), WIDE)
        c1 = [param(C1, pole, cols) for pole in range(2)]
        c2 = [param(C2, pole, cols) for pole in range(2)]
        now, old = [], []
        for pole in range(2):
            owner, there = message_place(b)
            cr = jnp.broadcast_to(c_in[owner, 0, pl.ds(pole, 1), there], (CHUNKS, WIDE))
            ci = jnp.broadcast_to(c_in[owner, 1, pl.ds(pole, 1), there], (CHUNKS, WIDE))
            for bit, wr, wi in ((1, RE16, IM16), (2, RE32, IM32), (4, RE64, IM64)):
                wr, wi = param(wr, pole, cols), param(wi, pole, cols)
                has = (sub & bit) > 0
                cr, ci = (
                    jnp.where(has, wr * cr - wi * ci, cr),
                    jnp.where(has, wr * ci + wi * cr, ci),
                )
            zr = scan[2 * pole, :, cols] + cr
            zi = scan[2 * pole + 1, :, cols] + ci
            old.append(param(G0, pole, cols) * zr + param(H1, pole, cols) * zi)
            now.append(param(H0R, pole, cols) * zr + param(H0I, pole, cols) * zi)
        done = []
        for r in range(steps):
            at = slice(CHUNKS * r, CHUNKS * (r + 1))
            done.append(query[at, cols] * (local[at, cols] + (now[0] + now[1])))
            for pole in range(2):
                now[pole], old[pole] = c2[pole] * old[pole] + c1[pole] * now[pole], now[pole]
        gated = jnp.concatenate(done, axis=0).astype(BF16)
        outs[:, cols] = jnp.dot(to_rows[...], gated, preferred_element_type=F32).astype(BF16)
        out_copy(b).start()
        return carry

    lax.fori_loop(0, blocks, pass_c, 0, unroll=2)

    def wait_out(b, carry):
        out_copy(b).wait()
        return carry

    lax.fori_loop(0, blocks, wait_out, 0)

    for step in range(1, members):
        t_copy(place, peer(step)).wait_send()
        c_copy(place, peer(step)).wait_send()
    pl.when(has_group_after)(chain_copy.wait_send)
    pl.when(me < n - 1)(halo_copy.wait_send)


def solution(mesh):
    n = mesh.shape["seq"]

    def on_device(projected, short_taps, skip_gain, residues, pole_angles, decay_rates):
        _, rows, width = projected.shape
        members = math.gcd(n, 4)
        quarter = width // members
        kv_parts = 4
        dma = pltpu.SemaphoreType.DMA
        vmem = pltpu.VMEM
        return pl.pallas_call(
            functools.partial(kernel, n, members),
            out_shape=jax.ShapeDtypeStruct((rows, width), BF16),
            in_specs=[pl.BlockSpec(memory_space=pl.ANY)] * 6,
            out_specs=pl.BlockSpec(memory_space=pl.ANY),
            scratch_shapes=[
                vmem((3, rows, width), BF16),
                vmem((3, rows, width), F32),
                vmem((3, 16, width), BF16),
                vmem(short_taps.shape, F32),
                vmem((1, width), F32),
                vmem(residues.shape, F32),
                vmem(pole_angles.shape, F32),
                vmem(decay_rates.shape, F32),
                vmem((rows, rows), BF16),
                vmem((rows, rows), BF16),
                vmem((TABLE_ROWS, 2, width), F32),
                vmem((16, width // 2), F32),
                vmem((16, width // 2), BF16),
                vmem((16, width // 2), BF16),
                vmem((8, width), F32),
                vmem((rows, width), F32),
                vmem((rows, width), F32),
                vmem((rows, width), F32),
                vmem((4, CHUNKS, width), F32),
                vmem((members, 2, 2, quarter), F32),
                vmem((members, 2, 2, quarter), F32),
                vmem((members, 2, 2, quarter), F32),
                vmem((members, 2, 2, quarter), F32),
                vmem((2, 2, quarter), F32),
                vmem((2, 2, quarter), F32),
                vmem((rows, width), BF16),
                dma((7,)),
                dma((kv_parts,)),
                dma((width // WIDE,)),
                dma((2,)),
                dma((members,)),
                dma((members,)),
                dma((members,)),
                dma((members,)),
                dma((2,)),
                pltpu.SemaphoreType.REGULAR((2,)),
            ],
            compiler_params=pltpu.CompilerParams(
                collective_id=0, has_side_effects=True, vmem_limit_bytes=63 * 1024 * 1024
            ),
            cost_estimate=pl.CostEstimate(
                flops=60 * rows * width, bytes_accessed=8 * rows * width, transcendentals=2 * width
            ),
        )(projected, short_taps, skip_gain.reshape(1, width), residues, pole_angles, decay_rates)

    return jax.shard_map(
        on_device,
        mesh=mesh,
        in_specs=(P(None, ("grp", "seq"), None), P(), P(), P(), P(), P()),
        out_specs=P(("grp", "seq"), None),
        check_vma=False,
    )
```

```python
import functools
import math

import jax
import jax.numpy as jnp
from jax import lax
from jax.experimental import pallas as pl
from jax.experimental.pallas import tpu as pltpu
from jax.sharding import PartitionSpec as P

MESH = pl.DeviceIdType.MESH
CHUNKS = 8
WIDE = 256
F32 = jnp.float32
BF16 = jnp.bfloat16

RE1, IM1, C1, C2, RE16, IM16, RE32, IM32, RE64, IM64, RE128, IM128, G0, G1, H1, H0R, H0I = range(17)
TABLE_ROWS = 17


def square(re, im):
    return re * re - im * im, 2.0 * (re * im)


def cos_sin_half(angle):
    x = 0.5 * angle
    z = x * x
    s = 1.0 / 6227020800.0
    for coefficient in (-1.0 / 39916800.0, 1.0 / 362880.0, -1.0 / 5040.0, 1.0 / 120.0, -1.0 / 6.0, 1.0):
        s = s * z + coefficient
    c = -1.0 / 87178291200.0
    for coefficient in (1.0 / 479001600.0, -1.0 / 3628800.0, 1.0 / 40320.0, -1.0 / 720.0, 1.0 / 24.0, -0.5, 1.0):
        c = c * z + coefficient
    return c, s * x


def kernel(
    n, members,
    x_hbm, taps_hbm, skip_hbm, res_hbm, ang_hbm, dec_hbm, out_hbm,
    xs, ordered, tail, taps, skip, res, ang, dec, to_chunks, to_rows, tab,
    halo_f32, halo_send, halo_recv, halo,
    prod, local, query, scan, t_send, t_in, c_out, c_in, g_out, g_in, outs,
    in_sems, kv_sems, out_sems, halo_sems, t_ssem, t_rsem, c_ssem, c_rsem, g_ssem, g_rsem, ready, halo_ready,
):
    rows, width = xs.shape[1], xs.shape[2]
    steps = rows // CHUNKS
    half_width = width // 2
    blocks = width // WIDE
    kv_parts = kv_sems.shape[0]
    part_width = width // kv_parts
    quarter = width // members
    me = lax.axis_index("seq")
    place = lax.rem(me, members)
    base = me - place
    groups = n // members
    group = base // members
    has_group_before = base > 0
    has_group_after = base + members < n
    is_first = place == 0
    is_last = place == members - 1

    def peer(step):
        other = place + step
        return jnp.where(other >= members, other - members, other)

    barrier = pltpu.get_barrier_semaphore()

    def signal(semaphore, device):
        pl.semaphore_signal(semaphore, inc=1, device_id={"seq": device}, device_id_type=MESH)

    for step in range(1, members):
        signal(barrier, base + peer(step))

    def in_later_groups(action):
        for ahead in range(1, groups):
            pl.when(group + ahead < groups)(functools.partial(action, ahead))

    in_later_groups(lambda ahead: signal(barrier, me + ahead * members))

    @pl.when(has_group_after & is_last)
    def _():
        signal(barrier, me + 1)

    def kv_copy(part):
        cols = pl.ds(pl.multiple_of(part * part_width, part_width), part_width)
        return pltpu.make_async_copy(
            x_hbm.at[pl.ds(1, 2), :, cols], xs.at[pl.ds(1, 2), :, cols], kv_sems.at[part]
        )

    tail_copy = pltpu.make_async_copy(
        x_hbm.at[:, pl.ds(rows - 16, 16), :], tail, in_sems.at[0]
    )
    tail_copy.start()
    small = [
        pltpu.make_async_copy(source, target, in_sems.at[1 + i])
        for i, (source, target) in enumerate(
            [(ang_hbm, ang), (dec_hbm, dec), (res_hbm, res), (taps_hbm, taps), (skip_hbm, skip)]
        )
    ]
    for copy in small:
        copy.start()
    for part in range(kv_parts):
        kv_copy(part).start()
    q_copy = pltpu.make_async_copy(x_hbm.at[0], xs.at[0], in_sems.at[6])
    q_copy.start()

    i0 = lax.broadcasted_iota(jnp.int32, (rows, rows), 0)
    i1 = lax.broadcasted_iota(jnp.int32, (rows, rows), 1)
    to_chunks[...] = jnp.where(i1 == (i0 & (CHUNKS - 1)) * steps + (i0 >> 3), 1.0, 0.0).astype(BF16)
    to_rows[...] = jnp.where(i0 == (i1 & (CHUNKS - 1)) * steps + (i1 >> 3), 1.0, 0.0).astype(BF16)

    tail_copy.wait()
    for i in range(3):
        last = tail[i].astype(F32)[14:16]
        halo_f32[2 * i : 2 * i + 2, :] = last[:, :half_width]
        halo_f32[8 + 2 * i : 10 + 2 * i, :] = last[:, half_width:]
    halo_f32[6:8, :] = jnp.zeros((2, half_width), F32)
    halo_f32[14:16, :] = jnp.zeros((2, half_width), F32)
    halo_send[...] = halo_f32[...].astype(BF16)
    halo_copy = pltpu.make_async_remote_copy(
        src_ref=halo_send,
        dst_ref=halo_recv,
        send_sem=halo_sems.at[0],
        recv_sem=halo_sems.at[1],
        device_id={"seq": jnp.where(me < n - 1, me + 1, 0)},
        device_id_type=MESH,
    )
    for copy in small:
        copy.wait()

    def parameters(b, carry):
        cols = pl.ds(pl.multiple_of(b * part_width, part_width), part_width)
        c, s = cos_sin_half(ang[:, cols])
        root = jnp.exp(-0.5 * dec[:, cols])
        re, im = square(root * c, root * s)
        r0, r1 = res[0, :, cols], res[1, :, cols]
        tab[RE1, :, cols] = re
        tab[IM1, :, cols] = im
        tab[C1, :, cols] = 2.0 * re
        tab[C2, :, cols] = -(re * re + im * im)
        tab[G0, :, cols] = r0
        tab[G1, :, cols] = -(r0 * re + r1 * im)
        tab[H1, :, cols] = -r1
        tab[H0R, :, cols] = r0 * re - r1 * im
        tab[H0I, :, cols] = -(r0 * im + r1 * re)
        power = 1
        while power < rows:
            re, im = square(re, im)
            power *= 2
            if power == steps:
                tab[RE16, :, cols], tab[IM16, :, cols] = re, im
            elif power == 2 * steps:
                tab[RE32, :, cols], tab[IM32, :, cols] = re, im
            elif power == 4 * steps:
                tab[RE64, :, cols], tab[IM64, :, cols] = re, im
            elif power == 8 * steps:
                tab[RE128, :, cols], tab[IM128, :, cols] = re, im
        return carry

    lax.fori_loop(0, kv_parts, parameters, 0)
    first_of_later = jnp.where(has_group_before & is_first, 1, 0)
    pl.semaphore_wait(barrier, members - 1 + group + first_of_later)

    for back in range(1, groups):
        @pl.when(group >= back)
        def _():
            signal(ready.at[back], me - back * members)

    @pl.when(has_group_before & is_first)
    def _():
        signal(halo_ready, me - 1)

    @pl.when(has_group_after & is_last)
    def _():
        pl.semaphore_wait(halo_ready, 1)

    pl.when(me < n - 1)(halo_copy.start)

    def order(i, part):
        cols = pl.ds(pl.multiple_of(part * part_width, part_width), part_width)
        ordered[i, :, cols] = jnp.dot(to_chunks[...], xs[i, :, cols], preferred_element_type=F32)

    def order_kv(part, carry):
        kv_copy(part).wait()
        order(1, part)
        order(2, part)
        return carry

    lax.fori_loop(0, kv_parts, order_kv, 0)

    pl.when(me > 0)(halo_copy.wait_recv)
    keep = me > 0
    received = halo_recv[...].astype(F32)
    received = jnp.where(keep, received, jnp.zeros_like(received))
    halo[:, 0:half_width] = received[0:8]
    halo[:, half_width:width] = received[8:16]

    sub = lax.broadcasted_iota(jnp.int32, (CHUNKS, WIDE), 0)
    first = sub == 0

    def param(which, pole, cols):
        return jnp.broadcast_to(tab[which, pole : pole + 1, cols], (CHUNKS, WIDE))

    def short(i, cols):
        at = [ordered[i, CHUNKS * r : CHUNKS * (r + 1), cols] for r in range(steps)]
        before2 = jnp.where(first, halo[2 * i : 2 * i + 1, cols], pltpu.roll(at[steps - 2], 1, 0))
        before1 = jnp.where(first, halo[2 * i + 1 : 2 * i + 2, cols], pltpu.roll(at[steps - 1], 1, 0))
        at = [before2, before1] + at
        w = [jnp.broadcast_to(taps[tap, i : i + 1, cols], (CHUNKS, WIDE)) for tap in range(3)]
        return [w[0] * at[r] + w[1] * at[r + 1] + w[2] * at[r + 2] for r in range(steps)]

    def message_place(b):
        each = quarter // WIDE
        owner = b // each
        return owner, pl.ds(pl.multiple_of((b - owner * each) * WIDE, WIDE), WIDE)

    def pass_a(b, carry):
        cols = pl.ds(pl.multiple_of(b * WIDE, WIDE), WIDE)
        key = short(1, cols)
        value = short(2, cols)
        c1 = [param(C1, pole, cols) for pole in range(2)]
        c2 = [param(C2, pole, cols) for pole in range(2)]
        now = [jnp.zeros((CHUNKS, WIDE), F32)] * 2
        old = [jnp.zeros((CHUNKS, WIDE), F32)] * 2
        for r in range(steps):
            p = key[r] * value[r]
            prod[CHUNKS * r : CHUNKS * (r + 1), cols] = p
            for pole in range(2):
                now[pole], old[pole] = (p + c2[pole] * old[pole]) + c1[pole] * now[pole], now[pole]
        for pole in range(2):
            re = now[pole] - param(RE1, pole, cols) * old[pole]
            im = param(IM1, pole, cols) * old[pole]
            for shift, wr, wi in ((1, RE16, IM16), (2, RE32, IM32), (4, RE64, IM64)):
                wr, wi = param(wr, pole, cols), param(wi, pole, cols)
                far = sub >= shift
                pr = jnp.where(far, pltpu.roll(re, shift, 0), 0.0)
                pi = jnp.where(far, pltpu.roll(im, shift, 0), 0.0)
                re, im = re + (wr * pr - wi * pi), im + (wr * pi + wi * pr)
            scan[2 * pole, :, cols] = jnp.where(first, 0.0, pltpu.roll(re, 1, 0))
            scan[2 * pole + 1, :, cols] = jnp.where(first, 0.0, pltpu.roll(im, 1, 0))
            owner, there = message_place(b)
            t_send[owner, 0, pl.ds(pole, 1), there] = re[CHUNKS - 1 : CHUNKS]
            t_send[owner, 1, pl.ds(pole, 1), there] = im[CHUNKS - 1 : CHUNKS]
        return carry

    lax.fori_loop(0, blocks, pass_a, 0, unroll=2)

    def t_copy(source, target):
        return pltpu.make_async_remote_copy(
            src_ref=t_send.at[target],
            dst_ref=t_in.at[source],
            send_sem=t_ssem.at[target],
            recv_sem=t_rsem.at[source],
            device_id={"seq": base + target},
            device_id_type=MESH,
        )

    def c_copy(source, target):
        return pltpu.make_async_remote_copy(
            src_ref=c_out.at[target],
            dst_ref=c_in.at[source],
            send_sem=c_ssem.at[target],
            recv_sem=c_rsem.at[source],
            device_id={"seq": base + target},
            device_id_type=MESH,
        )

    def g_copy(source, ahead):
        return pltpu.make_async_remote_copy(
            src_ref=g_out,
            dst_ref=g_in.at[source],
            send_sem=g_ssem.at[ahead],
            recv_sem=g_rsem.at[source],
            device_id={"seq": lax.rem(me + ahead * members, n)},
            device_id_type=MESH,
        )

    for step in range(1, members):
        t_copy(place, peer(step)).start()

    q_copy.wait()

    def order_q(part, carry):
        order(0, part)
        return carry

    lax.fori_loop(0, kv_parts, order_q, 0)

    def pass_b(b, carry):
        cols = pl.ds(pl.multiple_of(b * WIDE, WIDE), WIDE)
        for r, values in enumerate(short(0, cols)):
            query[CHUNKS * r : CHUNKS * (r + 1), cols] = values
        return carry

    def pass_b2(b, carry):
        cols = pl.ds(pl.multiple_of(b * WIDE, WIDE), WIDE)
        c1 = [param(C1, pole, cols) for pole in range(2)]
        c2 = [param(C2, pole, cols) for pole in range(2)]
        g0 = [param(G0, pole, cols) for pole in range(2)]
        g1 = [param(G1, pole, cols) for pole in range(2)]
        gain = jnp.broadcast_to(skip[:, cols], (CHUNKS, WIDE))
        zero = jnp.zeros((CHUNKS, WIDE), F32)
        now, old, before = [zero] * 2, [zero] * 2, zero
        for r in range(steps):
            p = prod[CHUNKS * r : CHUNKS * (r + 1), cols]
            for pole in range(2):
                fresh = ((g0[pole] * p + g1[pole] * before) + c2[pole] * old[pole]) + c1[pole] * now[pole]
                now[pole], old[pole] = fresh, now[pole]
            local[CHUNKS * r : CHUNKS * (r + 1), cols] = now[0] + now[1] + gain * p
            before = p
        return carry

    lax.fori_loop(0, blocks, pass_b, 0, unroll=2)

    t_in[pl.ds(place, 1)] = t_send[pl.ds(place, 1)]
    for step in range(1, members):
        t_copy(peer(step), place).wait_recv()

    mine = pl.ds(pl.multiple_of(place * quarter, quarter), quarter)
    wr, wi = tab[RE128, :, mine], tab[IM128, :, mine]
    re = im = jnp.zeros((2, quarter), F32)
    inside = []
    for member in range(members):
        inside.append((re, im))
        re, im = (
            wr * re - wi * im + t_in[member, 0],
            wr * im + wi * re + t_in[member, 1],
        )
    g_out[0] = re
    g_out[1] = im

    def send_g(ahead):
        pl.semaphore_wait(ready.at[ahead], 1)
        g_copy(group, ahead).start()

    in_later_groups(send_g)

    gr, gi = wr, wi
    span = 1
    while span < members:
        gr, gi = square(gr, gi)
        span *= 2

    def add_group(source, state):
        re, im = state
        g_copy(source, 1).wait_recv()
        return gr * re - gi * im + g_in[source, 0], gr * im + gi * re + g_in[source, 1]

    zero = jnp.zeros((2, quarter), F32)
    re, im = lax.fori_loop(0, group, add_group, (zero, zero))
    for member in range(members):
        c_out[member, 0] = inside[member][0] + re
        c_out[member, 1] = inside[member][1] + im
        re, im = wr * re - wi * im, wr * im + wi * re

    for step in range(1, members):
        c_copy(place, peer(step)).start()
    c_in[pl.ds(place, 1)] = c_out[pl.ds(place, 1)]

    lax.fori_loop(0, blocks, pass_b2, 0, unroll=2)

    for step in range(1, members):
        c_copy(peer(step), place).wait_recv()

    def out_copy(b):
        cols = pl.ds(pl.multiple_of(b * WIDE, WIDE), WIDE)
        return pltpu.make_async_copy(outs.at[:, cols], out_hbm.at[:, cols], out_sems.at[b])

    def pass_c(b, carry):
        cols = pl.ds(pl.multiple_of(b * WIDE, WIDE), WIDE)
        c1 = [param(C1, pole, cols) for pole in range(2)]
        c2 = [param(C2, pole, cols) for pole in range(2)]
        now, old = [], []
        for pole in range(2):
            owner, there = message_place(b)
            cr = jnp.broadcast_to(c_in[owner, 0, pl.ds(pole, 1), there], (CHUNKS, WIDE))
            ci = jnp.broadcast_to(c_in[owner, 1, pl.ds(pole, 1), there], (CHUNKS, WIDE))
            for bit, wr, wi in ((1, RE16, IM16), (2, RE32, IM32), (4, RE64, IM64)):
                wr, wi = param(wr, pole, cols), param(wi, pole, cols)
                has = (sub & bit) > 0
                cr, ci = (
                    jnp.where(has, wr * cr - wi * ci, cr),
                    jnp.where(has, wr * ci + wi * cr, ci),
                )
            zr = scan[2 * pole, :, cols] + cr
            zi = scan[2 * pole + 1, :, cols] + ci
            old.append(param(G0, pole, cols) * zr + param(H1, pole, cols) * zi)
            now.append(param(H0R, pole, cols) * zr + param(H0I, pole, cols) * zi)
        done = []
        for r in range(steps):
            at = slice(CHUNKS * r, CHUNKS * (r + 1))
            done.append(query[at, cols] * (local[at, cols] + (now[0] + now[1])))
            for pole in range(2):
                now[pole], old[pole] = c2[pole] * old[pole] + c1[pole] * now[pole], now[pole]
        gated = jnp.concatenate(done, axis=0).astype(BF16)
        outs[:, cols] = jnp.dot(to_rows[...], gated, preferred_element_type=F32).astype(BF16)
        out_copy(b).start()
        return carry

    lax.fori_loop(0, blocks, pass_c, 0, unroll=2)

    def wait_out(b, carry):
        out_copy(b).wait()
        return carry

    lax.fori_loop(0, blocks, wait_out, 0)

    for step in range(1, members):
        t_copy(place, peer(step)).wait_send()
        c_copy(place, peer(step)).wait_send()
    in_later_groups(lambda ahead: g_copy(group, ahead).wait_send())
    pl.when(me < n - 1)(halo_copy.wait_send)


def solution(mesh):
    n = mesh.shape["seq"]

    def on_device(projected, short_taps, skip_gain, residues, pole_angles, decay_rates):
        _, rows, width = projected.shape
        members = math.gcd(n, 4)
        quarter = width // members
        groups = n // members
        kv_parts = 4
        dma = pltpu.SemaphoreType.DMA
        vmem = pltpu.VMEM
        return pl.pallas_call(
            functools.partial(kernel, n, members),
            out_shape=jax.ShapeDtypeStruct((rows, width), BF16),
            in_specs=[pl.BlockSpec(memory_space=pl.ANY)] * 6,
            out_specs=pl.BlockSpec(memory_space=pl.ANY),
            scratch_shapes=[
                vmem((3, rows, width), BF16),
                vmem((3, rows, width), F32),
                vmem((3, 16, width), BF16),
                vmem(short_taps.shape, F32),
                vmem((1, width), F32),
                vmem(residues.shape, F32),
                vmem(pole_angles.shape, F32),
                vmem(decay_rates.shape, F32),
                vmem((rows, rows), BF16),
                vmem((rows, rows), BF16),
                vmem((TABLE_ROWS, 2, width), F32),
                vmem((16, width // 2), F32),
                vmem((16, width // 2), BF16),
                vmem((16, width // 2), BF16),
                vmem((8, width), F32),
                vmem((rows, width), F32),
                vmem((rows, width), F32),
                vmem((rows, width), F32),
                vmem((4, CHUNKS, width), F32),
                vmem((members, 2, 2, quarter), F32),
                vmem((members, 2, 2, quarter), F32),
                vmem((members, 2, 2, quarter), F32),
                vmem((members, 2, 2, quarter), F32),
                vmem((2, 2, quarter), F32),
                vmem((groups, 2, 2, quarter), F32),
                vmem((rows, width), BF16),
                dma((7,)),
                dma((kv_parts,)),
                dma((width // WIDE,)),
                dma((2,)),
                dma((members,)),
                dma((members,)),
                dma((members,)),
                dma((members,)),
                dma((groups,)),
                dma((groups,)),
                pltpu.SemaphoreType.REGULAR((groups,)),
                pltpu.SemaphoreType.REGULAR,
            ],
            compiler_params=pltpu.CompilerParams(
                collective_id=0, has_side_effects=True, vmem_limit_bytes=52 * 1024 * 1024
            ),
            cost_estimate=pl.CostEstimate(
                flops=60 * rows * width, bytes_accessed=8 * rows * width, transcendentals=2 * width
            ),
        )(projected, short_taps, skip_gain.reshape(1, width), residues, pole_angles, decay_rates)

    return jax.shard_map(
        on_device,
        mesh=mesh,
        in_specs=(P(None, ("grp", "seq"), None), P(), P(), P(), P(), P()),
        out_specs=P(("grp", "seq"), None),
        check_vma=False,
    )
```

```python
import functools
import math

import jax
import jax.numpy as jnp
from jax import lax
from jax.experimental import pallas as pl
from jax.experimental.pallas import tpu as pltpu
from jax.sharding import PartitionSpec as P

MESH = pl.DeviceIdType.MESH
CHUNKS = 8
WIDE = 256
F32 = jnp.float32
BF16 = jnp.bfloat16

RE1, IM1, C1, C2, RE16, IM16, RE32, IM32, RE64, IM64, RE128, IM128, G0, G1, H1, H0R, H0I, INVR, INVI = range(19)
TABLE_ROWS = 19


def square(re, im):
    return re * re - im * im, 2.0 * (re * im)


def cos_sin_half(angle):
    x = 0.5 * angle
    z = x * x
    s = 1.0 / 6227020800.0
    for coefficient in (-1.0 / 39916800.0, 1.0 / 362880.0, -1.0 / 5040.0, 1.0 / 120.0, -1.0 / 6.0, 1.0):
        s = s * z + coefficient
    c = -1.0 / 87178291200.0
    for coefficient in (1.0 / 479001600.0, -1.0 / 3628800.0, 1.0 / 40320.0, -1.0 / 720.0, 1.0 / 24.0, -0.5, 1.0):
        c = c * z + coefficient
    return c, s * x


def kernel(
    n, members,
    x_hbm, taps_hbm, skip_hbm, res_hbm, ang_hbm, dec_hbm, out_hbm,
    xs, delta, tail, taps, skip, res, ang, dec, to_chunks, to_rows, tab,
    halo_f32, halo_send, halo_recv, halo,
    prod, local, query, scan, t_send, t_in, c_out, c_in, g_out, g_in, outs,
    in_sems, kv_sems, out_sems, halo_sems, t_ssem, t_rsem, c_ssem, c_rsem, g_ssem, g_rsem, ready, halo_ready,
):
    rows, width = xs.shape[1], xs.shape[2]
    steps = rows // CHUNKS
    half_width = width // 2
    blocks = width // WIDE
    kv_parts = kv_sems.shape[0]
    part_width = width // kv_parts
    quarter = width // members
    me = lax.axis_index("seq")
    place = lax.rem(me, members)
    base = me - place
    groups = n // members
    group = base // members
    has_group_before = base > 0
    has_group_after = base + members < n
    is_first = place == 0
    is_last = place == members - 1

    def peer(step):
        other = place + step
        return jnp.where(other >= members, other - members, other)

    barrier = pltpu.get_barrier_semaphore()

    def signal(semaphore, device):
        pl.semaphore_signal(semaphore, inc=1, device_id={"seq": device}, device_id_type=MESH)

    for step in range(1, members):
        signal(barrier, base + peer(step))

    def in_later_groups(action):
        for ahead in range(1, groups):
            pl.when(group + ahead < groups)(functools.partial(action, ahead))

    in_later_groups(lambda ahead: signal(barrier, me + ahead * members))

    @pl.when(has_group_after & is_last)
    def _():
        signal(barrier, me + 1)

    def kv_copy(part):
        cols = pl.ds(pl.multiple_of(part * part_width, part_width), part_width)
        return pltpu.make_async_copy(
            x_hbm.at[pl.ds(1, 2), :, cols], xs.at[pl.ds(1, 2), :, cols], kv_sems.at[part]
        )

    tail_copy = pltpu.make_async_copy(
        x_hbm.at[:, pl.ds(rows - 16, 16), :], tail, in_sems.at[0]
    )
    tail_copy.start()
    small = [
        pltpu.make_async_copy(source, target, in_sems.at[1 + i])
        for i, (source, target) in enumerate(
            [(ang_hbm, ang), (dec_hbm, dec), (res_hbm, res), (taps_hbm, taps), (skip_hbm, skip)]
        )
    ]
    for copy in small:
        copy.start()
    for part in range(kv_parts):
        kv_copy(part).start()
    q_copy = pltpu.make_async_copy(x_hbm.at[0], xs.at[0], in_sems.at[6])
    q_copy.start()

    i0 = lax.broadcasted_iota(jnp.int32, (rows, rows), 0)
    i1 = lax.broadcasted_iota(jnp.int32, (rows, rows), 1)
    to_chunks[...] = jnp.where(i1 == (i0 & (CHUNKS - 1)) * steps + (i0 >> 3), 1.0, 0.0).astype(BF16)
    to_rows[...] = jnp.where(i0 == (i1 & (CHUNKS - 1)) * steps + (i1 >> 3), 1.0, 0.0).astype(BF16)

    tail_copy.wait()
    for i in range(3):
        last = tail[i].astype(F32)[14:16]
        halo_f32[2 * i : 2 * i + 2, :] = last[:, :half_width]
        halo_f32[8 + 2 * i : 10 + 2 * i, :] = last[:, half_width:]
    halo_f32[6:8, :] = jnp.zeros((2, half_width), F32)
    halo_f32[14:16, :] = jnp.zeros((2, half_width), F32)
    halo_send[...] = halo_f32[...].astype(BF16)
    halo_copy = pltpu.make_async_remote_copy(
        src_ref=halo_send,
        dst_ref=halo_recv,
        send_sem=halo_sems.at[0],
        recv_sem=halo_sems.at[1],
        device_id={"seq": jnp.where(me < n - 1, me + 1, 0)},
        device_id_type=MESH,
    )
    for copy in small:
        copy.wait()

    def parameters(b, carry):
        cols = pl.ds(pl.multiple_of(b * part_width, part_width), part_width)
        c, s = cos_sin_half(ang[:, cols])
        root = jnp.exp(-0.5 * dec[:, cols])
        re, im = square(root * c, root * s)
        r0, r1 = res[0, :, cols], res[1, :, cols]
        tab[RE1, :, cols] = re
        tab[IM1, :, cols] = im
        tab[C1, :, cols] = 2.0 * re
        size = re * re + im * im
        tab[C2, :, cols] = -size
        tab[INVR, :, cols] = re / size
        tab[INVI, :, cols] = -im / size
        tab[G0, :, cols] = r0
        tab[G1, :, cols] = -(r0 * re + r1 * im)
        tab[H1, :, cols] = -r1
        tab[H0R, :, cols] = r0 * re - r1 * im
        tab[H0I, :, cols] = -(r0 * im + r1 * re)
        power = 1
        while power < rows:
            re, im = square(re, im)
            power *= 2
            if power == steps:
                tab[RE16, :, cols], tab[IM16, :, cols] = re, im
            elif power == 2 * steps:
                tab[RE32, :, cols], tab[IM32, :, cols] = re, im
            elif power == 4 * steps:
                tab[RE64, :, cols], tab[IM64, :, cols] = re, im
            elif power == 8 * steps:
                tab[RE128, :, cols], tab[IM128, :, cols] = re, im
        return carry

    lax.fori_loop(0, kv_parts, parameters, 0)
    first_of_later = jnp.where(has_group_before & is_first, 1, 0)
    pl.semaphore_wait(barrier, members - 1 + group + first_of_later)

    for back in range(1, groups):
        @pl.when(group >= back)
        def _():
            signal(ready.at[back], me - back * members)

    @pl.when(has_group_before & is_first)
    def _():
        signal(halo_ready, me - 1)

    @pl.when(has_group_after & is_last)
    def _():
        pl.semaphore_wait(halo_ready, 1)

    pl.when(me < n - 1)(halo_copy.start)

    sub = lax.broadcasted_iota(jnp.int32, (CHUNKS, WIDE), 0)
    first = sub == 0

    def param(which, pole, cols):
        return jnp.broadcast_to(tab[which, pole : pole + 1, cols], (CHUNKS, WIDE))

    def short(i, cols, edge):
        x = jnp.dot(to_chunks[...], xs[i, :, cols], preferred_element_type=F32)
        at = [x[CHUNKS * r : CHUNKS * (r + 1)] for r in range(steps)]
        before2 = jnp.where(first, edge[0], pltpu.roll(at[steps - 2], 1, 0))
        before1 = jnp.where(first, edge[1], pltpu.roll(at[steps - 1], 1, 0))
        at = [before2, before1] + at
        w = [jnp.broadcast_to(taps[tap, i : i + 1, cols], (CHUNKS, WIDE)) for tap in range(3)]
        return [w[0] * at[r] + w[1] * at[r + 1] + w[2] * at[r + 2] for r in range(steps)]

    def message_place(b):
        each = quarter // WIDE
        owner = b // each
        return owner, pl.ds(pl.multiple_of((b - owner * each) * WIDE, WIDE), WIDE)

    def pass_a(b, carry):
        cols = pl.ds(pl.multiple_of(b * WIDE, WIDE), WIDE)
        key = short(1, cols, (0.0, 0.0))
        value = short(2, cols, (0.0, 0.0))
        c1 = [param(C1, pole, cols) for pole in range(2)]
        c2 = [param(C2, pole, cols) for pole in range(2)]
        now = [jnp.zeros((CHUNKS, WIDE), F32)] * 2
        old = [jnp.zeros((CHUNKS, WIDE), F32)] * 2
        for r in range(steps):
            p = key[r] * value[r]
            prod[CHUNKS * r : CHUNKS * (r + 1), cols] = p
            for pole in range(2):
                now[pole], old[pole] = (p + c2[pole] * old[pole]) + c1[pole] * now[pole], now[pole]
        for pole in range(2):
            re = now[pole] - param(RE1, pole, cols) * old[pole]
            im = param(IM1, pole, cols) * old[pole]
            for shift, wr, wi in ((1, RE16, IM16), (2, RE32, IM32), (4, RE64, IM64)):
                wr, wi = param(wr, pole, cols), param(wi, pole, cols)
                far = sub >= shift
                pr = jnp.where(far, pltpu.roll(re, shift, 0), 0.0)
                pi = jnp.where(far, pltpu.roll(im, shift, 0), 0.0)
                re, im = re + (wr * pr - wi * pi), im + (wr * pi + wi * pr)
            scan[2 * pole, :, cols] = jnp.where(first, 0.0, pltpu.roll(re, 1, 0))
            scan[2 * pole + 1, :, cols] = jnp.where(first, 0.0, pltpu.roll(im, 1, 0))
            owner, there = message_place(b)
            t_send[owner, 0, pl.ds(pole, 1), there] = re[CHUNKS - 1 : CHUNKS]
            t_send[owner, 1, pl.ds(pole, 1), there] = im[CHUNKS - 1 : CHUNKS]
        return carry

    def part_a(part, carry):
        kv_copy(part).wait()
        each = part_width // WIDE
        return lax.fori_loop(0, each, lambda b, c: pass_a(part * each + b, c), carry, unroll=2)

    lax.fori_loop(0, kv_parts, part_a, 0)

    pl.when(me > 0)(halo_copy.wait_recv)
    keep = me > 0
    received = halo_recv[...].astype(F32)
    received = jnp.where(keep, received, jnp.zeros_like(received))
    halo[:, 0:half_width] = received[0:8]
    halo[:, half_width:width] = received[8:16]

    def fix(owner, carry):
        cols = pl.ds(pl.multiple_of(owner * quarter, quarter), quarter)
        right = [1.0, 1.0]
        for i in (1, 2):
            x = xs[i, 0:16, cols].astype(F32)
            x0, x1 = x[0:1], x[1:2]
            h0, h1 = halo[2 * i : 2 * i + 1, cols], halo[2 * i + 1 : 2 * i + 2, cols]
            w = [taps[tap, i : i + 1, cols] for tap in range(3)]
            right[0] = right[0] * (w[0] * h0 + w[1] * h1 + w[2] * x0)
            right[1] = right[1] * (w[0] * h1 + w[1] * x0 + w[2] * x1)
        d0 = right[0] - prod[0:1, cols]
        d1 = right[1] - prod[CHUNKS : CHUNKS + 1, cols]
        prod[0:1, cols] = right[0]
        prod[CHUNKS : CHUNKS + 1, cols] = right[1]
        inv_r, inv_i = tab[INVR, :, cols], tab[INVI, :, cols]
        re, im = d0 + inv_r * d1, inv_i * d1
        re, im = inv_r * re - inv_i * im, inv_r * im + inv_i * re
        delta[0, :, cols] = re
        delta[1, :, cols] = im
        wr, wi = tab[RE128, :, cols], tab[IM128, :, cols]
        t_send[owner, 0] += wr * re - wi * im
        t_send[owner, 1] += wr * im + wi * re
        return carry

    lax.fori_loop(0, members, fix, 0)

    def t_copy(source, target):
        return pltpu.make_async_remote_copy(
            src_ref=t_send.at[target],
            dst_ref=t_in.at[source],
            send_sem=t_ssem.at[target],
            recv_sem=t_rsem.at[source],
            device_id={"seq": base + target},
            device_id_type=MESH,
        )

    def c_copy(source, target):
        return pltpu.make_async_remote_copy(
            src_ref=c_out.at[target],
            dst_ref=c_in.at[source],
            send_sem=c_ssem.at[target],
            recv_sem=c_rsem.at[source],
            device_id={"seq": base + target},
            device_id_type=MESH,
        )

    def g_copy(source, ahead):
        return pltpu.make_async_remote_copy(
            src_ref=g_out,
            dst_ref=g_in.at[source],
            send_sem=g_ssem.at[ahead],
            recv_sem=g_rsem.at[source],
            device_id={"seq": lax.rem(me + ahead * members, n)},
            device_id_type=MESH,
        )

    for step in range(1, members):
        t_copy(place, peer(step)).start()

    q_copy.wait()

    def pass_b(b, carry):
        cols = pl.ds(pl.multiple_of(b * WIDE, WIDE), WIDE)
        for r, values in enumerate(short(0, cols, (halo[0:1, cols], halo[1:2, cols]))):
            query[CHUNKS * r : CHUNKS * (r + 1), cols] = values
        return carry

    def pass_b2(b, carry):
        cols = pl.ds(pl.multiple_of(b * WIDE, WIDE), WIDE)
        c1 = [param(C1, pole, cols) for pole in range(2)]
        c2 = [param(C2, pole, cols) for pole in range(2)]
        g0 = [param(G0, pole, cols) for pole in range(2)]
        g1 = [param(G1, pole, cols) for pole in range(2)]
        gain = jnp.broadcast_to(skip[:, cols], (CHUNKS, WIDE))
        zero = jnp.zeros((CHUNKS, WIDE), F32)
        now, old, before = [zero] * 2, [zero] * 2, zero
        for r in range(steps):
            p = prod[CHUNKS * r : CHUNKS * (r + 1), cols]
            for pole in range(2):
                fresh = ((g0[pole] * p + g1[pole] * before) + c2[pole] * old[pole]) + c1[pole] * now[pole]
                now[pole], old[pole] = fresh, now[pole]
            local[CHUNKS * r : CHUNKS * (r + 1), cols] = now[0] + now[1] + gain * p
            before = p
        return carry

    lax.fori_loop(0, blocks, pass_b, 0, unroll=2)

    t_in[pl.ds(place, 1)] = t_send[pl.ds(place, 1)]
    for step in range(1, members):
        t_copy(peer(step), place).wait_recv()

    mine = pl.ds(pl.multiple_of(place * quarter, quarter), quarter)
    wr, wi = tab[RE128, :, mine], tab[IM128, :, mine]
    re = im = jnp.zeros((2, quarter), F32)
    inside = []
    for member in range(members):
        inside.append((re, im))
        re, im = (
            wr * re - wi * im + t_in[member, 0],
            wr * im + wi * re + t_in[member, 1],
        )
    g_out[0] = re
    g_out[1] = im

    def send_g(ahead):
        pl.semaphore_wait(ready.at[ahead], 1)
        g_copy(group, ahead).start()

    in_later_groups(send_g)

    gr, gi = wr, wi
    span = 1
    while span < members:
        gr, gi = square(gr, gi)
        span *= 2

    def add_group(source, state):
        re, im = state
        g_copy(source, 1).wait_recv()
        return gr * re - gi * im + g_in[source, 0], gr * im + gi * re + g_in[source, 1]

    zero = jnp.zeros((2, quarter), F32)
    re, im = lax.fori_loop(0, group, add_group, (zero, zero))
    for member in range(members):
        c_out[member, 0] = inside[member][0] + re
        c_out[member, 1] = inside[member][1] + im
        re, im = wr * re - wi * im, wr * im + wi * re

    for step in range(1, members):
        c_copy(place, peer(step)).start()
    c_in[pl.ds(place, 1)] = c_out[pl.ds(place, 1)]

    lax.fori_loop(0, blocks, pass_b2, 0, unroll=2)

    for step in range(1, members):
        c_copy(peer(step), place).wait_recv()

    def out_copy(b):
        cols = pl.ds(pl.multiple_of(b * WIDE, WIDE), WIDE)
        return pltpu.make_async_copy(outs.at[:, cols], out_hbm.at[:, cols], out_sems.at[b])

    def pass_c(b, carry):
        cols = pl.ds(pl.multiple_of(b * WIDE, WIDE), WIDE)
        c1 = [param(C1, pole, cols) for pole in range(2)]
        c2 = [param(C2, pole, cols) for pole in range(2)]
        now, old = [], []
        for pole in range(2):
            owner, there = message_place(b)
            cr = jnp.broadcast_to(c_in[owner, 0, pl.ds(pole, 1), there], (CHUNKS, WIDE))
            ci = jnp.broadcast_to(c_in[owner, 1, pl.ds(pole, 1), there], (CHUNKS, WIDE))
            dr = jnp.broadcast_to(delta[0, pole : pole + 1, cols], (CHUNKS, WIDE))
            di = jnp.broadcast_to(delta[1, pole : pole + 1, cols], (CHUNKS, WIDE))
            cr, ci = jnp.where(first, cr, cr + dr), jnp.where(first, ci, ci + di)
            for bit, wr, wi in ((1, RE16, IM16), (2, RE32, IM32), (4, RE64, IM64)):
                wr, wi = param(wr, pole, cols), param(wi, pole, cols)
                has = (sub & bit) > 0
                cr, ci = (
                    jnp.where(has, wr * cr - wi * ci, cr),
                    jnp.where(has, wr * ci + wi * cr, ci),
                )
            zr = scan[2 * pole, :, cols] + cr
            zi = scan[2 * pole + 1, :, cols] + ci
            old.append(param(G0, pole, cols) * zr + param(H1, pole, cols) * zi)
            now.append(param(H0R, pole, cols) * zr + param(H0I, pole, cols) * zi)
        done = []
        for r in range(steps):
            at = slice(CHUNKS * r, CHUNKS * (r + 1))
            done.append(query[at, cols] * (local[at, cols] + (now[0] + now[1])))
            for pole in range(2):
                now[pole], old[pole] = c2[pole] * old[pole] + c1[pole] * now[pole], now[pole]
        gated = jnp.concatenate(done, axis=0).astype(BF16)
        outs[:, cols] = jnp.dot(to_rows[...], gated, preferred_element_type=F32)
        out_copy(b).start()
        return carry

    lax.fori_loop(0, blocks, pass_c, 0, unroll=2)

    def wait_out(b, carry):
        out_copy(b).wait()
        return carry

    lax.fori_loop(0, blocks, wait_out, 0)

    for step in range(1, members):
        t_copy(place, peer(step)).wait_send()
        c_copy(place, peer(step)).wait_send()
    in_later_groups(lambda ahead: g_copy(group, ahead).wait_send())
    pl.when(me < n - 1)(halo_copy.wait_send)


def solution(mesh):
    n = mesh.shape["seq"]

    def on_device(projected, short_taps, skip_gain, residues, pole_angles, decay_rates):
        _, rows, width = projected.shape
        members = math.gcd(n, 4)
        quarter = width // members
        groups = n // members
        kv_parts = 4
        dma = pltpu.SemaphoreType.DMA
        vmem = pltpu.VMEM
        return pl.pallas_call(
            functools.partial(kernel, n, members),
            out_shape=jax.ShapeDtypeStruct((rows, width), F32),
            in_specs=[pl.BlockSpec(memory_space=pl.ANY)] * 6,
            out_specs=pl.BlockSpec(memory_space=pl.ANY),
            scratch_shapes=[
                vmem((3, rows, width), BF16),
                vmem((2, 2, width), F32),
                vmem((3, 16, width), BF16),
                vmem(short_taps.shape, F32),
                vmem((1, width), F32),
                vmem(residues.shape, F32),
                vmem(pole_angles.shape, F32),
                vmem(decay_rates.shape, F32),
                vmem((rows, rows), BF16),
                vmem((rows, rows), BF16),
                vmem((TABLE_ROWS, 2, width), F32),
                vmem((16, width // 2), F32),
                vmem((16, width // 2), BF16),
                vmem((16, width // 2), BF16),
                vmem((8, width), F32),
                vmem((rows, width), F32),
                vmem((rows, width), F32),
                vmem((rows, width), F32),
                vmem((4, CHUNKS, width), F32),
                vmem((members, 2, 2, quarter), F32),
                vmem((members, 2, 2, quarter), F32),
                vmem((members, 2, 2, quarter), F32),
                vmem((members, 2, 2, quarter), F32),
                vmem((2, 2, quarter), F32),
                vmem((groups, 2, 2, quarter), F32),
                vmem((rows, width), F32),
                dma((7,)),
                dma((kv_parts,)),
                dma((width // WIDE,)),
                dma((2,)),
                dma((members,)),
                dma((members,)),
                dma((members,)),
                dma((members,)),
                dma((groups,)),
                dma((groups,)),
                pltpu.SemaphoreType.REGULAR((groups,)),
                pltpu.SemaphoreType.REGULAR,
            ],
            compiler_params=pltpu.CompilerParams(
                collective_id=0, has_side_effects=True, vmem_limit_bytes=63 * 1024 * 1024
            ),
            cost_estimate=pl.CostEstimate(
                flops=60 * rows * width, bytes_accessed=8 * rows * width, transcendentals=2 * width
            ),
        )(projected, short_taps, skip_gain.reshape(1, width), residues, pole_angles, decay_rates).astype(BF16)

    return jax.shard_map(
        on_device,
        mesh=mesh,
        in_specs=(P(None, ("grp", "seq"), None), P(), P(), P(), P(), P()),
        out_specs=P(("grp", "seq"), None),
        check_vma=False,
    )
```

```python
import functools
import math

import jax
import jax.numpy as jnp
from jax import lax
from jax.experimental import pallas as pl
from jax.experimental.pallas import tpu as pltpu
from jax.sharding import PartitionSpec as P

MESH = pl.DeviceIdType.MESH
CHUNKS = 8
WIDE = 256
F32 = jnp.float32
BF16 = jnp.bfloat16

RE1, IM1, C1, C2, RE16, IM16, RE32, IM32, RE64, IM64, RE128, IM128, G0, G1, H1, H0R, H0I, INVR, INVI = range(19)
TABLE_ROWS = 19


def square(re, im):
    return re * re - im * im, 2.0 * (re * im)


def cos_sin_half(angle):
    x = 0.5 * angle
    z = x * x
    s = 1.0 / 6227020800.0
    for coefficient in (-1.0 / 39916800.0, 1.0 / 362880.0, -1.0 / 5040.0, 1.0 / 120.0, -1.0 / 6.0, 1.0):
        s = s * z + coefficient
    c = -1.0 / 87178291200.0
    for coefficient in (1.0 / 479001600.0, -1.0 / 3628800.0, 1.0 / 40320.0, -1.0 / 720.0, 1.0 / 24.0, -0.5, 1.0):
        c = c * z + coefficient
    return c, s * x


def kernel(
    n, members,
    x_hbm, taps_hbm, skip_hbm, res_hbm, ang_hbm, dec_hbm, out_hbm,
    xs, delta, tail, taps, skip, res, ang, dec, to_chunks, tab,
    halo_f32, halo_send, halo_recv, halo,
    prod, local, query, scan, state, spin, carried, t_send, t_in, c_out, c_in, g_out, g_in, outs,
    in_sems, kv_sems, out_sems, halo_sems, t_ssem, t_rsem, c_ssem, c_rsem, g_ssem, g_rsem, ready, halo_ready,
):
    rows, width = xs.shape[1], xs.shape[2]
    steps = rows // CHUNKS
    half_width = width // 2
    blocks = width // WIDE
    kv_parts = kv_sems.shape[0]
    part_width = width // kv_parts
    quarter = width // members
    pieces = quarter // WIDE
    half = 2 * pieces
    me = lax.axis_index("seq")
    place = lax.rem(me, members)
    base = me - place
    groups = n // members
    group = base // members
    has_group_before = base > 0
    has_group_after = base + members < n
    is_first = place == 0
    is_last = place == members - 1

    def peer(step):
        other = place + step
        return jnp.where(other >= members, other - members, other)

    barrier = pltpu.get_barrier_semaphore()

    def signal(semaphore, device):
        pl.semaphore_signal(semaphore, inc=1, device_id={"seq": device}, device_id_type=MESH)

    for step in range(1, members):
        signal(barrier, base + peer(step))

    def in_later_groups(action):
        for ahead in range(1, groups):
            pl.when(group + ahead < groups)(functools.partial(action, ahead))

    in_later_groups(lambda ahead: signal(barrier, me + ahead * members))

    @pl.when(has_group_after & is_last)
    def _():
        signal(barrier, me + 1)

    def kv_copy(part):
        cols = pl.ds(pl.multiple_of(part * part_width, part_width), part_width)
        return pltpu.make_async_copy(
            x_hbm.at[pl.ds(1, 2), :, cols], xs.at[pl.ds(1, 2), :, cols], kv_sems.at[part]
        )

    tail_copy = pltpu.make_async_copy(
        x_hbm.at[:, pl.ds(rows - 16, 16), :], tail, in_sems.at[0]
    )
    tail_copy.start()
    small = [
        pltpu.make_async_copy(source, target, in_sems.at[1 + i])
        for i, (source, target) in enumerate(
            [(ang_hbm, ang), (dec_hbm, dec), (res_hbm, res), (taps_hbm, taps), (skip_hbm, skip)]
        )
    ]
    for copy in small:
        copy.start()
    for part in range(kv_parts):
        kv_copy(part).start()
    q_copy = pltpu.make_async_copy(x_hbm.at[0], xs.at[0], in_sems.at[6])
    q_copy.start()

    i0 = lax.broadcasted_iota(jnp.int32, (rows, rows), 0)
    i1 = lax.broadcasted_iota(jnp.int32, (rows, rows), 1)
    to_chunks[...] = jnp.where(i1 == (i0 & (CHUNKS - 1)) * steps + (i0 >> 3), 1.0, 0.0).astype(BF16)

    tail_copy.wait()
    for i in range(3):
        last = tail[i].astype(F32)[14:16]
        halo_f32[2 * i : 2 * i + 2, :] = last[:, :half_width]
        halo_f32[8 + 2 * i : 10 + 2 * i, :] = last[:, half_width:]
    halo_f32[6:8, :] = jnp.zeros((2, half_width), F32)
    halo_f32[14:16, :] = jnp.zeros((2, half_width), F32)
    halo_send[...] = halo_f32[...].astype(BF16)
    halo_copy = pltpu.make_async_remote_copy(
        src_ref=halo_send,
        dst_ref=halo_recv,
        send_sem=halo_sems.at[0],
        recv_sem=halo_sems.at[1],
        device_id={"seq": jnp.where(me < n - 1, me + 1, 0)},
        device_id_type=MESH,
    )
    for copy in small:
        copy.wait()

    def parameters(b, carry):
        cols = pl.ds(pl.multiple_of(b * part_width, part_width), part_width)
        c, s = cos_sin_half(ang[:, cols])
        root = jnp.exp(-0.5 * dec[:, cols])
        re, im = square(root * c, root * s)
        r0, r1 = res[0, :, cols], res[1, :, cols]
        tab[RE1, :, cols] = re
        tab[IM1, :, cols] = im
        tab[C1, :, cols] = 2.0 * re
        size = re * re + im * im
        tab[C2, :, cols] = -size
        tab[INVR, :, cols] = re / size
        tab[INVI, :, cols] = -im / size
        tab[G0, :, cols] = r0
        tab[G1, :, cols] = -(r0 * re + r1 * im)
        tab[H1, :, cols] = -r1
        tab[H0R, :, cols] = r0 * re - r1 * im
        tab[H0I, :, cols] = -(r0 * im + r1 * re)
        power = 1
        while power < rows:
            re, im = square(re, im)
            power *= 2
            if power == steps:
                tab[RE16, :, cols], tab[IM16, :, cols] = re, im
            elif power == 2 * steps:
                tab[RE32, :, cols], tab[IM32, :, cols] = re, im
            elif power == 4 * steps:
                tab[RE64, :, cols], tab[IM64, :, cols] = re, im
            elif power == 8 * steps:
                tab[RE128, :, cols], tab[IM128, :, cols] = re, im
        return carry

    lax.fori_loop(0, kv_parts, parameters, 0)
    first_of_later = jnp.where(has_group_before & is_first, 1, 0)
    pl.semaphore_wait(barrier, members - 1 + group + first_of_later)

    for back in range(1, groups):
        @pl.when(group >= back)
        def _():
            signal(ready.at[back], me - back * members)

    @pl.when(has_group_before & is_first)
    def _():
        signal(halo_ready, me - 1)

    @pl.when(has_group_after & is_last)
    def _():
        pl.semaphore_wait(halo_ready, 1)

    pl.when(me < n - 1)(halo_copy.start)

    sub = lax.broadcasted_iota(jnp.int32, (CHUNKS, WIDE), 0)
    first = sub == 0

    def param(which, pole, cols):
        return jnp.broadcast_to(tab[which, pole : pole + 1, cols], (CHUNKS, WIDE))

    def short(i, cols, edge):
        x = jnp.dot(to_chunks[...], xs[i, :, cols], preferred_element_type=F32)
        at = [x[CHUNKS * r : CHUNKS * (r + 1)] for r in range(steps)]
        before2 = jnp.where(first, edge[0], pltpu.roll(at[steps - 2], 1, 0))
        before1 = jnp.where(first, edge[1], pltpu.roll(at[steps - 1], 1, 0))
        at = [before2, before1] + at
        w = [jnp.broadcast_to(taps[tap, i : i + 1, cols], (CHUNKS, WIDE)) for tap in range(3)]
        return [w[0] * at[r] + w[1] * at[r + 1] + w[2] * at[r + 2] for r in range(steps)]

    def message_place(b):
        owner = b // pieces
        return owner, 2 * (b - owner * pieces)

    def pass_a(b, carry):
        cols = pl.ds(pl.multiple_of(b * WIDE, WIDE), WIDE)
        key = short(1, cols, (0.0, 0.0))
        value = short(2, cols, (0.0, 0.0))
        c1 = [param(C1, pole, cols) for pole in range(2)]
        c2 = [param(C2, pole, cols) for pole in range(2)]
        now = [jnp.zeros((CHUNKS, WIDE), F32)] * 2
        old = [jnp.zeros((CHUNKS, WIDE), F32)] * 2
        for r in range(steps):
            p = key[r] * value[r]
            prod[CHUNKS * r : CHUNKS * (r + 1), cols] = p
            for pole in range(2):
                now[pole], old[pole] = (p + c2[pole] * old[pole]) + c1[pole] * now[pole], now[pole]
        for pole in range(2):
            re = now[pole] - param(RE1, pole, cols) * old[pole]
            im = param(IM1, pole, cols) * old[pole]
            for shift, wr, wi in ((1, RE16, IM16), (2, RE32, IM32), (4, RE64, IM64)):
                wr, wi = param(wr, pole, cols), param(wi, pole, cols)
                far = sub >= shift
                pr = jnp.where(far, pltpu.roll(re, shift, 0), 0.0)
                pi = jnp.where(far, pltpu.roll(im, shift, 0), 0.0)
                re, im = re + (wr * pr - wi * pi), im + (wr * pi + wi * pr)
            scan[2 * pole, :, cols] = jnp.where(first, 0.0, pltpu.roll(re, 1, 0))
            scan[2 * pole + 1, :, cols] = jnp.where(first, 0.0, pltpu.roll(im, 1, 0))
            owner, row = message_place(b)
            state[owner, pl.ds(row + pole, 1), :] = re[CHUNKS - 1 : CHUNKS]
            state[owner, pl.ds(half + row + pole, 1), :] = im[CHUNKS - 1 : CHUNKS]
        return carry

    def part_a(part, carry):
        kv_copy(part).wait()
        each = part_width // WIDE
        return lax.fori_loop(0, each, lambda b, c: pass_a(part * each + b, c), carry, unroll=2)

    lax.fori_loop(0, kv_parts, part_a, 0)

    pl.when(me > 0)(halo_copy.wait_recv)
    keep = me > 0
    received = halo_recv[...].astype(F32)
    received = jnp.where(keep, received, jnp.zeros_like(received))
    halo[:, 0:half_width] = received[0:8]
    halo[:, half_width:width] = received[8:16]

    def fix(owner, carry):
        cols = pl.ds(pl.multiple_of(owner * quarter, quarter), quarter)
        right = [1.0, 1.0]
        for i in (1, 2):
            x = xs[i, 0:16, cols].astype(F32)
            x0, x1 = x[0:1], x[1:2]
            h0, h1 = halo[2 * i : 2 * i + 1, cols], halo[2 * i + 1 : 2 * i + 2, cols]
            w = [taps[tap, i : i + 1, cols] for tap in range(3)]
            right[0] = right[0] * (w[0] * h0 + w[1] * h1 + w[2] * x0)
            right[1] = right[1] * (w[0] * h1 + w[1] * x0 + w[2] * x1)
        d0 = right[0] - prod[0:1, cols]
        d1 = right[1] - prod[CHUNKS : CHUNKS + 1, cols]
        prod[0:1, cols] = right[0]
        prod[CHUNKS : CHUNKS + 1, cols] = right[1]
        inv_r, inv_i = tab[INVR, :, cols], tab[INVI, :, cols]
        re, im = d0 + inv_r * d1, inv_i * d1
        re, im = inv_r * re - inv_i * im, inv_r * im + inv_i * re
        delta[0, :, cols] = re
        delta[1, :, cols] = im
        wr, wi = tab[RE128, :, cols], tab[IM128, :, cols]
        add = (wr * re - wi * im, wr * im + wi * re)
        for part in range(2):
            for piece in range(pieces):
                row = part * half + 2 * piece
                state[owner, row : row + 2, :] += add[part][:, piece * WIDE : (piece + 1) * WIDE]
        t_send[owner] = state[owner].astype(BF16)
        return carry

    lax.fori_loop(0, members, fix, 0)

    def t_copy(source, target):
        return pltpu.make_async_remote_copy(
            src_ref=t_send.at[target],
            dst_ref=t_in.at[source],
            send_sem=t_ssem.at[target],
            recv_sem=t_rsem.at[source],
            device_id={"seq": base + target},
            device_id_type=MESH,
        )

    def c_copy(source, target):
        return pltpu.make_async_remote_copy(
            src_ref=c_out.at[target],
            dst_ref=c_in.at[source],
            send_sem=c_ssem.at[target],
            recv_sem=c_rsem.at[source],
            device_id={"seq": base + target},
            device_id_type=MESH,
        )

    def g_copy(source, ahead):
        return pltpu.make_async_remote_copy(
            src_ref=g_out,
            dst_ref=g_in.at[source],
            send_sem=g_ssem.at[ahead],
            recv_sem=g_rsem.at[source],
            device_id={"seq": lax.rem(me + ahead * members, n)},
            device_id_type=MESH,
        )

    for step in range(1, members):
        t_copy(place, peer(step)).start()

    q_copy.wait()

    def pass_b(b, carry):
        cols = pl.ds(pl.multiple_of(b * WIDE, WIDE), WIDE)
        for r, values in enumerate(short(0, cols, (halo[0:1, cols], halo[1:2, cols]))):
            query[CHUNKS * r : CHUNKS * (r + 1), cols] = values
        return carry

    def pass_b2(b, carry):
        cols = pl.ds(pl.multiple_of(b * WIDE, WIDE), WIDE)
        c1 = [param(C1, pole, cols) for pole in range(2)]
        c2 = [param(C2, pole, cols) for pole in range(2)]
        g0 = [param(G0, pole, cols) for pole in range(2)]
        g1 = [param(G1, pole, cols) for pole in range(2)]
        gain = jnp.broadcast_to(skip[:, cols], (CHUNKS, WIDE))
        zero = jnp.zeros((CHUNKS, WIDE), F32)
        now, old, before = [zero] * 2, [zero] * 2, zero
        for r in range(steps):
            p = prod[CHUNKS * r : CHUNKS * (r + 1), cols]
            for pole in range(2):
                fresh = ((g0[pole] * p + g1[pole] * before) + c2[pole] * old[pole]) + c1[pole] * now[pole]
                now[pole], old[pole] = fresh, now[pole]
            local[CHUNKS * r : CHUNKS * (r + 1), cols] = now[0] + now[1] + gain * p
            before = p
        return carry

    lax.fori_loop(0, blocks, pass_b, 0, unroll=2)

    t_in[pl.ds(place, 1)] = t_send[pl.ds(place, 1)]
    for piece in range(pieces):
        cols = pl.ds(pl.multiple_of(place * quarter + piece * WIDE, WIDE), WIDE)
        spin[0, 2 * piece : 2 * piece + 2, :] = tab[RE128, :, cols]
        spin[1, 2 * piece : 2 * piece + 2, :] = tab[IM128, :, cols]
    for step in range(1, members):
        t_copy(peer(step), place).wait_recv()

    wr, wi = spin[0], spin[1]
    re = im = jnp.zeros((half, WIDE), F32)
    inside = []
    for member in range(members):
        inside.append((re, im))
        ended = t_in[member].astype(F32)
        re, im = wr * re - wi * im + ended[:half], wr * im + wi * re + ended[half:]
    g_out[...] = jnp.concatenate([re, im], axis=0).astype(BF16)

    def send_g(ahead):
        pl.semaphore_wait(ready.at[ahead], 1)
        g_copy(group, ahead).start()

    in_later_groups(send_g)

    gr, gi = wr, wi
    span = 1
    while span < members:
        gr, gi = square(gr, gi)
        span *= 2

    def add_group(source, state):
        re, im = state
        g_copy(source, 1).wait_recv()
        ended = g_in[source].astype(F32)
        return gr * re - gi * im + ended[:half], gr * im + gi * re + ended[half:]

    zero = jnp.zeros((half, WIDE), F32)
    re, im = lax.fori_loop(0, group, add_group, (zero, zero))
    for member in range(members):
        c_out[member] = jnp.concatenate(
            [inside[member][0] + re, inside[member][1] + im], axis=0
        ).astype(BF16)
        re, im = wr * re - wi * im, wr * im + wi * re

    for step in range(1, members):
        c_copy(place, peer(step)).start()
    c_in[pl.ds(place, 1)] = c_out[pl.ds(place, 1)]

    lax.fori_loop(0, blocks, pass_b2, 0, unroll=2)

    for step in range(1, members):
        c_copy(peer(step), place).wait_recv()
    carried[...] = c_in[...].astype(F32)

    def out_copy(b):
        cols = pl.ds(pl.multiple_of(b * WIDE, WIDE), WIDE)
        return pltpu.make_async_copy(outs.at[:, cols], out_hbm.at[:, cols], out_sems.at[b])

    def pass_c(b, carry):
        cols = pl.ds(pl.multiple_of(b * WIDE, WIDE), WIDE)
        c1 = [param(C1, pole, cols) for pole in range(2)]
        c2 = [param(C2, pole, cols) for pole in range(2)]
        now, old = [], []
        for pole in range(2):
            owner, row = message_place(b)
            cr = jnp.broadcast_to(carried[owner, pl.ds(row + pole, 1), :], (CHUNKS, WIDE))
            ci = jnp.broadcast_to(carried[owner, pl.ds(half + row + pole, 1), :], (CHUNKS, WIDE))
            dr = jnp.broadcast_to(delta[0, pole : pole + 1, cols], (CHUNKS, WIDE))
            di = jnp.broadcast_to(delta[1, pole : pole + 1, cols], (CHUNKS, WIDE))
            cr, ci = jnp.where(first, cr, cr + dr), jnp.where(first, ci, ci + di)
            for bit, wr, wi in ((1, RE16, IM16), (2, RE32, IM32), (4, RE64, IM64)):
                wr, wi = param(wr, pole, cols), param(wi, pole, cols)
                has = (sub & bit) > 0
                cr, ci = (
                    jnp.where(has, wr * cr - wi * ci, cr),
                    jnp.where(has, wr * ci + wi * cr, ci),
                )
            zr = scan[2 * pole, :, cols] + cr
            zi = scan[2 * pole + 1, :, cols] + ci
            old.append(param(G0, pole, cols) * zr + param(H1, pole, cols) * zi)
            now.append(param(H0R, pole, cols) * zr + param(H0I, pole, cols) * zi)
        done = []
        for r in range(steps):
            at = slice(CHUNKS * r, CHUNKS * (r + 1))
            done.append(query[at, cols] * (local[at, cols] + (now[0] + now[1])))
            for pole in range(2):
                now[pole], old[pole] = c2[pole] * old[pole] + c1[pole] * now[pole], now[pole]
        gated = jnp.concatenate(done, axis=0).astype(BF16)
        outs[:, cols] = gated
        out_copy(b).start()
        return carry

    lax.fori_loop(0, blocks, pass_c, 0, unroll=2)

    def wait_out(b, carry):
        out_copy(b).wait()
        return carry

    lax.fori_loop(0, blocks, wait_out, 0)

    for step in range(1, members):
        t_copy(place, peer(step)).wait_send()
        c_copy(place, peer(step)).wait_send()
    in_later_groups(lambda ahead: g_copy(group, ahead).wait_send())
    pl.when(me < n - 1)(halo_copy.wait_send)


def rows_kernel(x_hbm, out_hbm, xs, outs, in_sems, out_sems):
    rows, width = xs.shape
    steps = rows // CHUNKS
    parts = in_sems.shape[0]
    each = width // parts
    places = [pl.ds(part * each, each) for part in range(parts)]
    ins = [
        pltpu.make_async_copy(x_hbm.at[:, cols], xs.at[:, cols], in_sems.at[part])
        for part, cols in enumerate(places)
    ]
    backs = [
        pltpu.make_async_copy(outs.at[:, cols], out_hbm.at[:, cols], out_sems.at[part])
        for part, cols in enumerate(places)
    ]
    for copy in ins:
        copy.start()
    i0 = lax.broadcasted_iota(jnp.int32, (rows, rows), 0)
    i1 = lax.broadcasted_iota(jnp.int32, (rows, rows), 1)
    to_rows = jnp.where(i0 == (i1 & (CHUNKS - 1)) * steps + (i1 >> 3), 1.0, 0.0).astype(BF16)
    for part, cols in enumerate(places):
        ins[part].wait()
        outs[:, cols] = jnp.dot(to_rows, xs[:, cols], preferred_element_type=F32).astype(BF16)
        backs[part].start()
    for copy in backs:
        copy.wait()


def solution(mesh):
    n = mesh.shape["seq"]

    def on_device(projected, short_taps, skip_gain, residues, pole_angles, decay_rates):
        _, rows, width = projected.shape
        members = math.gcd(n, 4)
        quarter = width // members
        groups = n // members
        message = 4 * quarter // WIDE
        kv_parts = 4
        dma = pltpu.SemaphoreType.DMA
        vmem = pltpu.VMEM
        in_chunks = pl.pallas_call(
            functools.partial(kernel, n, members),
            out_shape=jax.ShapeDtypeStruct((rows, width), BF16),
            in_specs=[pl.BlockSpec(memory_space=pl.ANY)] * 6,
            out_specs=pl.BlockSpec(memory_space=pl.ANY),
            scratch_shapes=[
                vmem((3, rows, width), BF16),
                vmem((2, 2, width), F32),
                vmem((3, 16, width), BF16),
                vmem(short_taps.shape, F32),
                vmem((1, width), F32),
                vmem(residues.shape, F32),
                vmem(pole_angles.shape, F32),
                vmem(decay_rates.shape, F32),
                vmem((rows, rows), BF16),
                vmem((TABLE_ROWS, 2, width), F32),
                vmem((16, width // 2), F32),
                vmem((16, width // 2), BF16),
                vmem((16, width // 2), BF16),
                vmem((8, width), F32),
                vmem((rows, width), F32),
                vmem((rows, width), F32),
                vmem((rows, width), F32),
                vmem((4, CHUNKS, width), F32),
                vmem((members, message, WIDE), F32),
                vmem((2, message // 2, WIDE), F32),
                vmem((members, message, WIDE), F32),
                vmem((members, message, WIDE), BF16),
                vmem((members, message, WIDE), BF16),
                vmem((members, message, WIDE), BF16),
                vmem((members, message, WIDE), BF16),
                vmem((message, WIDE), BF16),
                vmem((groups, message, WIDE), BF16),
                vmem((rows, width), BF16),
                dma((7,)),
                dma((kv_parts,)),
                dma((width // WIDE,)),
                dma((2,)),
                dma((members,)),
                dma((members,)),
                dma((members,)),
                dma((members,)),
                dma((groups,)),
                dma((groups,)),
                pltpu.SemaphoreType.REGULAR((groups,)),
                pltpu.SemaphoreType.REGULAR,
            ],
            compiler_params=pltpu.CompilerParams(
                collective_id=0, has_side_effects=True, vmem_limit_bytes=63 * 1024 * 1024
            ),
            cost_estimate=pl.CostEstimate(
                flops=60 * rows * width, bytes_accessed=8 * rows * width, transcendentals=2 * width
            ),
        )(projected, short_taps, skip_gain.reshape(1, width), residues, pole_angles, decay_rates)
        parts = 8
        return pl.pallas_call(
            rows_kernel,
            out_shape=jax.ShapeDtypeStruct((rows, width), BF16),
            in_specs=[pl.BlockSpec(memory_space=pl.ANY)],
            out_specs=pl.BlockSpec(memory_space=pl.ANY),
            scratch_shapes=[
                vmem((rows, width), BF16),
                vmem((rows, width), BF16),
                dma((parts,)),
                dma((parts,)),
            ],
            compiler_params=pltpu.CompilerParams(vmem_limit_bytes=63 * 1024 * 1024),
            cost_estimate=pl.CostEstimate(
                flops=2 * rows * rows * width, bytes_accessed=4 * rows * width, transcendentals=0
            ),
        )(in_chunks)

    return jax.shard_map(
        on_device,
        mesh=mesh,
        in_specs=(P(None, ("grp", "seq"), None), P(), P(), P(), P(), P()),
        out_specs=P(("grp", "seq"), None),
        check_vma=False,
    )
```

```python
import functools
import math

import jax
import jax.numpy as jnp
from jax import lax
from jax.experimental import pallas as pl
from jax.experimental.pallas import tpu as pltpu
from jax.sharding import PartitionSpec as P

MESH = pl.DeviceIdType.MESH
CHUNKS = 8
WIDE = 256
F32 = jnp.float32
BF16 = jnp.bfloat16

RE1, IM1, C1, C2, RE16, IM16, RE32, IM32, RE64, IM64, RE128, IM128, G0, G1, H1, H0R, H0I, INVR, INVI = range(19)
TABLE_ROWS = 19


def square(re, im):
    return re * re - im * im, 2.0 * (re * im)


def cos_sin_half(angle):
    x = 0.5 * angle
    z = x * x
    s = 1.0 / 6227020800.0
    for coefficient in (-1.0 / 39916800.0, 1.0 / 362880.0, -1.0 / 5040.0, 1.0 / 120.0, -1.0 / 6.0, 1.0):
        s = s * z + coefficient
    c = -1.0 / 87178291200.0
    for coefficient in (1.0 / 479001600.0, -1.0 / 3628800.0, 1.0 / 40320.0, -1.0 / 720.0, 1.0 / 24.0, -0.5, 1.0):
        c = c * z + coefficient
    return c, s * x


def kernel(
    n, members,
    x_hbm, taps_hbm, skip_hbm, res_hbm, ang_hbm, dec_hbm, out_hbm,
    xs, delta, tail, taps, skip, res, ang, dec, to_chunks, to_rows, tab,
    halo_f32, halo_send, halo_recv, halo,
    prod, local, query, scan, state, spin, carried, t_send, t_in, c_out, c_in, g_out, g_in, outs,
    in_sems, kv_sems, out_sems, halo_sems, t_ssem, t_rsem, c_ssem, c_rsem, g_ssem, g_rsem, ready, halo_ready,
):
    rows, width = xs.shape[1], xs.shape[2]
    steps = rows // CHUNKS
    half_width = width // 2
    blocks = width // WIDE
    kv_parts = kv_sems.shape[0]
    part_width = width // kv_parts
    quarter = width // members
    pieces = quarter // WIDE
    half = 2 * pieces
    me = lax.axis_index("seq")
    place = lax.rem(me, members)
    base = me - place
    groups = n // members
    group = base // members
    has_group_before = base > 0
    has_group_after = base + members < n
    is_first = place == 0
    is_last = place == members - 1

    def peer(step):
        other = place + step
        return jnp.where(other >= members, other - members, other)

    barrier = pltpu.get_barrier_semaphore()

    def signal(semaphore, device):
        pl.semaphore_signal(semaphore, inc=1, device_id={"seq": device}, device_id_type=MESH)

    for step in range(1, members):
        signal(barrier, base + peer(step))

    def in_later_groups(action):
        for ahead in range(1, groups):
            pl.when(group + ahead < groups)(functools.partial(action, ahead))

    in_later_groups(lambda ahead: signal(barrier, me + ahead * members))

    @pl.when(has_group_after & is_last)
    def _():
        signal(barrier, me + 1)

    def kv_copy(part):
        cols = pl.ds(pl.multiple_of(part * part_width, part_width), part_width)
        return pltpu.make_async_copy(
            x_hbm.at[pl.ds(1, 2), :, cols], xs.at[pl.ds(1, 2), :, cols], kv_sems.at[part]
        )

    tail_copy = pltpu.make_async_copy(
        x_hbm.at[:, pl.ds(rows - 16, 16), :], tail, in_sems.at[0]
    )
    tail_copy.start()
    small = [
        pltpu.make_async_copy(source, target, in_sems.at[1 + i])
        for i, (source, target) in enumerate(
            [(ang_hbm, ang), (dec_hbm, dec), (res_hbm, res), (taps_hbm, taps), (skip_hbm, skip)]
        )
    ]
    for copy in small:
        copy.start()
    for part in range(kv_parts):
        kv_copy(part).start()
    q_copy = pltpu.make_async_copy(x_hbm.at[0], xs.at[0], in_sems.at[6])
    q_copy.start()

    i0 = lax.broadcasted_iota(jnp.int32, (rows, rows), 0)
    i1 = lax.broadcasted_iota(jnp.int32, (rows, rows), 1)
    to_chunks[...] = jnp.where(i1 == (i0 & (CHUNKS - 1)) * steps + (i0 >> 3), 1.0, 0.0).astype(BF16)

    to_rows[...] = jnp.where(i0 == (i1 & (CHUNKS - 1)) * steps + (i1 >> 3), 1.0, 0.0).astype(BF16)

    tail_copy.wait()
    for i in range(3):
        last = tail[i].astype(F32)[14:16]
        halo_f32[2 * i : 2 * i + 2, :] = last[:, :half_width]
        halo_f32[8 + 2 * i : 10 + 2 * i, :] = last[:, half_width:]
    halo_f32[6:8, :] = jnp.zeros((2, half_width), F32)
    halo_f32[14:16, :] = jnp.zeros((2, half_width), F32)
    halo_send[...] = halo_f32[...].astype(BF16)
    halo_copy = pltpu.make_async_remote_copy(
        src_ref=halo_send,
        dst_ref=halo_recv,
        send_sem=halo_sems.at[0],
        recv_sem=halo_sems.at[1],
        device_id={"seq": jnp.where(me < n - 1, me + 1, 0)},
        device_id_type=MESH,
    )
    for copy in small:
        copy.wait()

    def parameters(b, carry):
        cols = pl.ds(pl.multiple_of(b * part_width, part_width), part_width)
        c, s = cos_sin_half(ang[:, cols])
        root = jnp.exp(-0.5 * dec[:, cols])
        re, im = square(root * c, root * s)
        r0, r1 = res[0, :, cols], res[1, :, cols]
        tab[RE1, :, cols] = re
        tab[IM1, :, cols] = im
        tab[C1, :, cols] = 2.0 * re
        size = re * re + im * im
        tab[C2, :, cols] = -size
        tab[INVR, :, cols] = re / size
        tab[INVI, :, cols] = -im / size
        tab[G0, :, cols] = r0
        tab[G1, :, cols] = -(r0 * re + r1 * im)
        tab[H1, :, cols] = -r1
        tab[H0R, :, cols] = r0 * re - r1 * im
        tab[H0I, :, cols] = -(r0 * im + r1 * re)
        power = 1
        while power < rows:
            re, im = square(re, im)
            power *= 2
            if power == steps:
                tab[RE16, :, cols], tab[IM16, :, cols] = re, im
            elif power == 2 * steps:
                tab[RE32, :, cols], tab[IM32, :, cols] = re, im
            elif power == 4 * steps:
                tab[RE64, :, cols], tab[IM64, :, cols] = re, im
            elif power == 8 * steps:
                tab[RE128, :, cols], tab[IM128, :, cols] = re, im
        return carry

    lax.fori_loop(0, kv_parts, parameters, 0)
    first_of_later = jnp.where(has_group_before & is_first, 1, 0)
    pl.semaphore_wait(barrier, members - 1 + group + first_of_later)

    for back in range(1, groups):
        @pl.when(group >= back)
        def _():
            signal(ready.at[back], me - back * members)

    @pl.when(has_group_before & is_first)
    def _():
        signal(halo_ready, me - 1)

    @pl.when(has_group_after & is_last)
    def _():
        pl.semaphore_wait(halo_ready, 1)

    pl.when(me < n - 1)(halo_copy.start)

    sub = lax.broadcasted_iota(jnp.int32, (CHUNKS, WIDE), 0)
    first = sub == 0

    def param(which, pole, cols):
        return jnp.broadcast_to(tab[which, pole : pole + 1, cols], (CHUNKS, WIDE))

    def short(i, cols, edge):
        x = jnp.dot(to_chunks[...], xs[i, :, cols], preferred_element_type=F32)
        at = [x[CHUNKS * r : CHUNKS * (r + 1)] for r in range(steps)]
        before2 = jnp.where(first, edge[0], pltpu.roll(at[steps - 2], 1, 0))
        before1 = jnp.where(first, edge[1], pltpu.roll(at[steps - 1], 1, 0))
        at = [before2, before1] + at
        w = [jnp.broadcast_to(taps[tap, i : i + 1, cols], (CHUNKS, WIDE)) for tap in range(3)]
        return [w[0] * at[r] + w[1] * at[r + 1] + w[2] * at[r + 2] for r in range(steps)]

    def message_place(b):
        owner = b // pieces
        return owner, 2 * (b - owner * pieces)

    def pass_a(b, carry):
        cols = pl.ds(pl.multiple_of(b * WIDE, WIDE), WIDE)
        key = short(1, cols, (0.0, 0.0))
        value = short(2, cols, (0.0, 0.0))
        c1 = [param(C1, pole, cols) for pole in range(2)]
        c2 = [param(C2, pole, cols) for pole in range(2)]
        now = [jnp.zeros((CHUNKS, WIDE), F32)] * 2
        old = [jnp.zeros((CHUNKS, WIDE), F32)] * 2
        for r in range(steps):
            p = key[r] * value[r]
            prod[CHUNKS * r : CHUNKS * (r + 1), cols] = p
            for pole in range(2):
                now[pole], old[pole] = (p + c2[pole] * old[pole]) + c1[pole] * now[pole], now[pole]
        for pole in range(2):
            re = now[pole] - param(RE1, pole, cols) * old[pole]
            im = param(IM1, pole, cols) * old[pole]
            for shift, wr, wi in ((1, RE16, IM16), (2, RE32, IM32), (4, RE64, IM64)):
                wr, wi = param(wr, pole, cols), param(wi, pole, cols)
                far = sub >= shift
                pr = jnp.where(far, pltpu.roll(re, shift, 0), 0.0)
                pi = jnp.where(far, pltpu.roll(im, shift, 0), 0.0)
                re, im = re + (wr * pr - wi * pi), im + (wr * pi + wi * pr)
            scan[2 * pole, :, cols] = jnp.where(first, 0.0, pltpu.roll(re, 1, 0))
            scan[2 * pole + 1, :, cols] = jnp.where(first, 0.0, pltpu.roll(im, 1, 0))
            owner, row = message_place(b)
            state[owner, pl.ds(row + pole, 1), :] = re[CHUNKS - 1 : CHUNKS]
            state[owner, pl.ds(half + row + pole, 1), :] = im[CHUNKS - 1 : CHUNKS]
        return carry

    def part_a(part, carry):
        kv_copy(part).wait()
        each = part_width // WIDE
        return lax.fori_loop(0, each, lambda b, c: pass_a(part * each + b, c), carry, unroll=2)

    lax.fori_loop(0, kv_parts, part_a, 0)

    pl.when(me > 0)(halo_copy.wait_recv)
    keep = me > 0
    received = halo_recv[...].astype(F32)
    received = jnp.where(keep, received, jnp.zeros_like(received))
    halo[:, 0:half_width] = received[0:8]
    halo[:, half_width:width] = received[8:16]

    def fix(owner, carry):
        cols = pl.ds(pl.multiple_of(owner * quarter, quarter), quarter)
        right = [1.0, 1.0]
        for i in (1, 2):
            x = xs[i, 0:16, cols].astype(F32)
            x0, x1 = x[0:1], x[1:2]
            h0, h1 = halo[2 * i : 2 * i + 1, cols], halo[2 * i + 1 : 2 * i + 2, cols]
            w = [taps[tap, i : i + 1, cols] for tap in range(3)]
            right[0] = right[0] * (w[0] * h0 + w[1] * h1 + w[2] * x0)
            right[1] = right[1] * (w[0] * h1 + w[1] * x0 + w[2] * x1)
        d0 = right[0] - prod[0:1, cols]
        d1 = right[1] - prod[CHUNKS : CHUNKS + 1, cols]
        prod[0:1, cols] = right[0]
        prod[CHUNKS : CHUNKS + 1, cols] = right[1]
        inv_r, inv_i = tab[INVR, :, cols], tab[INVI, :, cols]
        re, im = d0 + inv_r * d1, inv_i * d1
        re, im = inv_r * re - inv_i * im, inv_r * im + inv_i * re
        delta[0, :, cols] = re
        delta[1, :, cols] = im
        wr, wi = tab[RE128, :, cols], tab[IM128, :, cols]
        add = (wr * re - wi * im, wr * im + wi * re)
        for part in range(2):
            for piece in range(pieces):
                row = part * half + 2 * piece
                state[owner, row : row + 2, :] += add[part][:, piece * WIDE : (piece + 1) * WIDE]
        t_send[owner] = state[owner].astype(BF16)
        return carry

    lax.fori_loop(0, members, fix, 0)

    def t_copy(source, target):
        return pltpu.make_async_remote_copy(
            src_ref=t_send.at[target],
            dst_ref=t_in.at[source],
            send_sem=t_ssem.at[target],
            recv_sem=t_rsem.at[source],
            device_id={"seq": base + target},
            device_id_type=MESH,
        )

    def c_copy(source, target):
        return pltpu.make_async_remote_copy(
            src_ref=c_out.at[target],
            dst_ref=c_in.at[source],
            send_sem=c_ssem.at[target],
            recv_sem=c_rsem.at[source],
            device_id={"seq": base + target},
            device_id_type=MESH,
        )

    def g_copy(source, ahead):
        return pltpu.make_async_remote_copy(
            src_ref=g_out,
            dst_ref=g_in.at[source],
            send_sem=g_ssem.at[ahead],
            recv_sem=g_rsem.at[source],
            device_id={"seq": lax.rem(me + ahead * members, n)},
            device_id_type=MESH,
        )

    for step in range(1, members):
        t_copy(place, peer(step)).start()

    q_copy.wait()

    def pass_b(b, carry):
        cols = pl.ds(pl.multiple_of(b * WIDE, WIDE), WIDE)
        for r, values in enumerate(short(0, cols, (halo[0:1, cols], halo[1:2, cols]))):
            query[CHUNKS * r : CHUNKS * (r + 1), cols] = values
        return carry

    def pass_b2(b, carry):
        cols = pl.ds(pl.multiple_of(b * WIDE, WIDE), WIDE)
        c1 = [param(C1, pole, cols) for pole in range(2)]
        c2 = [param(C2, pole, cols) for pole in range(2)]
        g0 = [param(G0, pole, cols) for pole in range(2)]
        g1 = [param(G1, pole, cols) for pole in range(2)]
        gain = jnp.broadcast_to(skip[:, cols], (CHUNKS, WIDE))
        zero = jnp.zeros((CHUNKS, WIDE), F32)
        now, old, before = [zero] * 2, [zero] * 2, zero
        for r in range(steps):
            p = prod[CHUNKS * r : CHUNKS * (r + 1), cols]
            for pole in range(2):
                fresh = ((g0[pole] * p + g1[pole] * before) + c2[pole] * old[pole]) + c1[pole] * now[pole]
                now[pole], old[pole] = fresh, now[pole]
            local[CHUNKS * r : CHUNKS * (r + 1), cols] = now[0] + now[1] + gain * p
            before = p
        return carry

    lax.fori_loop(0, blocks, pass_b, 0, unroll=2)

    t_in[pl.ds(place, 1)] = t_send[pl.ds(place, 1)]
    for piece in range(pieces):
        cols = pl.ds(pl.multiple_of(place * quarter + piece * WIDE, WIDE), WIDE)
        spin[0, 2 * piece : 2 * piece + 2, :] = tab[RE128, :, cols]
        spin[1, 2 * piece : 2 * piece + 2, :] = tab[IM128, :, cols]
    for step in range(1, members):
        t_copy(peer(step), place).wait_recv()

    wr, wi = spin[0], spin[1]
    re = im = jnp.zeros((half, WIDE), F32)
    inside = []
    for member in range(members):
        inside.append((re, im))
        ended = t_in[member].astype(F32)
        re, im = wr * re - wi * im + ended[:half], wr * im + wi * re + ended[half:]
    g_out[...] = jnp.concatenate([re, im], axis=0).astype(BF16)

    def send_g(ahead):
        pl.semaphore_wait(ready.at[ahead], 1)
        g_copy(group, ahead).start()

    in_later_groups(send_g)

    gr, gi = wr, wi
    span = 1
    while span < members:
        gr, gi = square(gr, gi)
        span *= 2

    def add_group(source, state):
        re, im = state
        g_copy(source, 1).wait_recv()
        ended = g_in[source].astype(F32)
        return gr * re - gi * im + ended[:half], gr * im + gi * re + ended[half:]

    zero = jnp.zeros((half, WIDE), F32)
    re, im = lax.fori_loop(0, group, add_group, (zero, zero))
    for member in range(members):
        c_out[member] = jnp.concatenate(
            [inside[member][0] + re, inside[member][1] + im], axis=0
        ).astype(BF16)
        re, im = wr * re - wi * im, wr * im + wi * re

    for step in range(1, members):
        c_copy(place, peer(step)).start()
    c_in[pl.ds(place, 1)] = c_out[pl.ds(place, 1)]

    lax.fori_loop(0, blocks, pass_b2, 0, unroll=2)

    for step in range(1, members):
        c_copy(peer(step), place).wait_recv()
    carried[...] = c_in[...].astype(F32)

    def out_copy(b):
        cols = pl.ds(pl.multiple_of(b * WIDE, WIDE), WIDE)
        return pltpu.make_async_copy(outs.at[:, cols], out_hbm.at[:, cols], out_sems.at[b])

    def pass_c(b, carry):
        cols = pl.ds(pl.multiple_of(b * WIDE, WIDE), WIDE)
        c1 = [param(C1, pole, cols) for pole in range(2)]
        c2 = [param(C2, pole, cols) for pole in range(2)]
        now, old = [], []
        for pole in range(2):
            owner, row = message_place(b)
            cr = jnp.broadcast_to(carried[owner, pl.ds(row + pole, 1), :], (CHUNKS, WIDE))
            ci = jnp.broadcast_to(carried[owner, pl.ds(half + row + pole, 1), :], (CHUNKS, WIDE))
            dr = jnp.broadcast_to(delta[0, pole : pole + 1, cols], (CHUNKS, WIDE))
            di = jnp.broadcast_to(delta[1, pole : pole + 1, cols], (CHUNKS, WIDE))
            cr, ci = jnp.where(first, cr, cr + dr), jnp.where(first, ci, ci + di)
            for bit, wr, wi in ((1, RE16, IM16), (2, RE32, IM32), (4, RE64, IM64)):
                wr, wi = param(wr, pole, cols), param(wi, pole, cols)
                has = (sub & bit) > 0
                cr, ci = (
                    jnp.where(has, wr * cr - wi * ci, cr),
                    jnp.where(has, wr * ci + wi * cr, ci),
                )
            zr = scan[2 * pole, :, cols] + cr
            zi = scan[2 * pole + 1, :, cols] + ci
            old.append(param(G0, pole, cols) * zr + param(H1, pole, cols) * zi)
            now.append(param(H0R, pole, cols) * zr + param(H0I, pole, cols) * zi)
        done = []
        for r in range(steps):
            at = slice(CHUNKS * r, CHUNKS * (r + 1))
            done.append(query[at, cols] * (local[at, cols] + (now[0] + now[1])))
            for pole in range(2):
                now[pole], old[pole] = c2[pole] * old[pole] + c1[pole] * now[pole], now[pole]
        gated = jnp.concatenate(done, axis=0).astype(BF16)
        outs[:, cols] = jnp.dot(to_rows[...], gated, preferred_element_type=F32).astype(BF16)
        out_copy(b).start()
        return carry

    lax.fori_loop(0, blocks, pass_c, 0, unroll=2)

    def wait_out(b, carry):
        out_copy(b).wait()
        return carry

    lax.fori_loop(0, blocks, wait_out, 0)

    for step in range(1, members):
        t_copy(place, peer(step)).wait_send()
        c_copy(place, peer(step)).wait_send()
    in_later_groups(lambda ahead: g_copy(group, ahead).wait_send())
    pl.when(me < n - 1)(halo_copy.wait_send)


def solution(mesh):
    n = mesh.shape["seq"]

    def on_device(projected, short_taps, skip_gain, residues, pole_angles, decay_rates):
        _, rows, width = projected.shape
        members = math.gcd(n, 4)
        quarter = width // members
        groups = n // members
        message = 4 * quarter // WIDE
        kv_parts = 4
        dma = pltpu.SemaphoreType.DMA
        vmem = pltpu.VMEM
        return pl.pallas_call(
            functools.partial(kernel, n, members),
            out_shape=pltpu.VMEM((rows, width), BF16),
            in_specs=[pl.BlockSpec(memory_space=pl.ANY)] * 6,
            out_specs=pl.BlockSpec(memory_space=pl.ANY),
            scratch_shapes=[
                vmem((3, rows, width), BF16),
                vmem((2, 2, width), F32),
                vmem((3, 16, width), BF16),
                vmem(short_taps.shape, F32),
                vmem((1, width), F32),
                vmem(residues.shape, F32),
                vmem(pole_angles.shape, F32),
                vmem(decay_rates.shape, F32),
                vmem((rows, rows), BF16),
                vmem((rows, rows), BF16),
                vmem((TABLE_ROWS, 2, width), F32),
                vmem((16, width // 2), F32),
                vmem((16, width // 2), BF16),
                vmem((16, width // 2), BF16),
                vmem((8, width), F32),
                vmem((rows, width), F32),
                vmem((rows, width), F32),
                vmem((rows, width), F32),
                vmem((4, CHUNKS, width), F32),
                vmem((members, message, WIDE), F32),
                vmem((2, message // 2, WIDE), F32),
                vmem((members, message, WIDE), F32),
                vmem((members, message, WIDE), BF16),
                vmem((members, message, WIDE), BF16),
                vmem((members, message, WIDE), BF16),
                vmem((members, message, WIDE), BF16),
                vmem((message, WIDE), BF16),
                vmem((groups, message, WIDE), BF16),
                vmem((rows, width), BF16),
                dma((7,)),
                dma((kv_parts,)),
                dma((width // WIDE,)),
                dma((2,)),
                dma((members,)),
                dma((members,)),
                dma((members,)),
                dma((members,)),
                dma((groups,)),
                dma((groups,)),
                pltpu.SemaphoreType.REGULAR((groups,)),
                pltpu.SemaphoreType.REGULAR,
            ],
            compiler_params=pltpu.CompilerParams(
                collective_id=0, has_side_effects=True, vmem_limit_bytes=40 * 1024 * 1024
            ),
            cost_estimate=pl.CostEstimate(
                flops=60 * rows * width, bytes_accessed=8 * rows * width, transcendentals=2 * width
            ),
        )(
            *[
                pltpu.with_memory_space_constraint(x, pltpu.HBM)
                for x in (
                    projected, short_taps, skip_gain.reshape(1, width), residues, pole_angles, decay_rates
                )
            ]
        )

    return jax.shard_map(
        on_device,
        mesh=mesh,
        in_specs=(P(None, ("grp", "seq"), None), P(), P(), P(), P(), P()),
        out_specs=P(("grp", "seq"), None),
        check_vma=False,
    )
```

```python
import functools
import math

import jax
import jax.numpy as jnp
from jax import lax
from jax.experimental import pallas as pl
from jax.experimental.pallas import tpu as pltpu
from jax.sharding import PartitionSpec as P

MESH = pl.DeviceIdType.MESH
CHUNKS = 8
WIDE = 256
F32 = jnp.float32
BF16 = jnp.bfloat16

RE1, IM1, C1, C2, RE16, IM16, RE32, IM32, RE64, IM64, RE128, IM128, G0, G1, H1, H0R, H0I, INVR, INVI = range(19)
TABLE_ROWS = 19


def square(re, im):
    return re * re - im * im, 2.0 * (re * im)


def cos_sin_half(angle):
    x = 0.5 * angle
    z = x * x
    s = 1.0 / 6227020800.0
    for coefficient in (-1.0 / 39916800.0, 1.0 / 362880.0, -1.0 / 5040.0, 1.0 / 120.0, -1.0 / 6.0, 1.0):
        s = s * z + coefficient
    c = -1.0 / 87178291200.0
    for coefficient in (1.0 / 479001600.0, -1.0 / 3628800.0, 1.0 / 40320.0, -1.0 / 720.0, 1.0 / 24.0, -0.5, 1.0):
        c = c * z + coefficient
    return c, s * x


def kernel(
    n, members,
    x_hbm, taps_hbm, skip_hbm, res_hbm, ang_hbm, dec_hbm, out_hbm,
    xs, even, odd, gated_even, gated_odd, delta, tail, taps, skip, res, ang, dec, to_chunks, to_rows, tab,
    halo_f32, halo_send, halo_recv, halo,
    prod, local, query, scan, state, spin, carried, t_send, t_in, c_out, c_in, g_out, g_in, outs,
    in_sems, kv_sems, out_sems, halo_sems, t_ssem, t_rsem, c_ssem, c_rsem, g_ssem, g_rsem, ready, halo_ready,
):
    rows, width = xs.shape[1], xs.shape[2]
    steps = rows // CHUNKS
    half_width = width // 2
    blocks = width // WIDE
    kv_parts = kv_sems.shape[0]
    part_width = width // kv_parts
    quarter = width // members
    pieces = quarter // WIDE
    half = 2 * pieces
    me = lax.axis_index("seq")
    place = lax.rem(me, members)
    base = me - place
    groups = n // members
    group = base // members
    has_group_before = base > 0
    has_group_after = base + members < n
    is_first = place == 0
    is_last = place == members - 1

    def peer(step):
        other = place + step
        return jnp.where(other >= members, other - members, other)

    barrier = pltpu.get_barrier_semaphore()

    def signal(semaphore, device):
        pl.semaphore_signal(semaphore, inc=1, device_id={"seq": device}, device_id_type=MESH)

    for step in range(1, members):
        signal(barrier, base + peer(step))

    def in_later_groups(action):
        for ahead in range(1, groups):
            pl.when(group + ahead < groups)(functools.partial(action, ahead))

    in_later_groups(lambda ahead: signal(barrier, me + ahead * members))

    @pl.when(has_group_after & is_last)
    def _():
        signal(barrier, me + 1)

    def kv_copy(part):
        cols = pl.ds(pl.multiple_of(part * part_width, part_width), part_width)
        return pltpu.make_async_copy(
            x_hbm.at[pl.ds(1, 2), :, cols], xs.at[pl.ds(1, 2), :, cols], kv_sems.at[part]
        )

    tail_copy = pltpu.make_async_copy(
        x_hbm.at[:, pl.ds(rows - 16, 16), :], tail, in_sems.at[0]
    )
    tail_copy.start()
    small = [
        pltpu.make_async_copy(source, target, in_sems.at[1 + i])
        for i, (source, target) in enumerate(
            [(ang_hbm, ang), (dec_hbm, dec), (res_hbm, res), (taps_hbm, taps), (skip_hbm, skip)]
        )
    ]
    for copy in small:
        copy.start()
    for part in range(kv_parts):
        kv_copy(part).start()
    q_copy = pltpu.make_async_copy(x_hbm.at[0], xs.at[0], in_sems.at[6])
    q_copy.start()

    i0 = lax.broadcasted_iota(jnp.int32, (rows, rows), 0)
    i1 = lax.broadcasted_iota(jnp.int32, (rows, rows), 1)
    to_chunks[...] = jnp.where(i1 == (i0 & (CHUNKS - 1)) * steps + (i0 >> 3), 1.0, 0.0).astype(BF16)

    to_rows[...] = jnp.where(i0 == (i1 & (CHUNKS - 1)) * steps + (i1 >> 3), 1.0, 0.0).astype(BF16)

    tail_copy.wait()
    for i in range(3):
        last = tail[i].astype(F32)[14:16]
        halo_f32[2 * i : 2 * i + 2, :] = last[:, :half_width]
        halo_f32[8 + 2 * i : 10 + 2 * i, :] = last[:, half_width:]
    halo_f32[6:8, :] = jnp.zeros((2, half_width), F32)
    halo_f32[14:16, :] = jnp.zeros((2, half_width), F32)
    halo_send[...] = halo_f32[...].astype(BF16)
    halo_copy = pltpu.make_async_remote_copy(
        src_ref=halo_send,
        dst_ref=halo_recv,
        send_sem=halo_sems.at[0],
        recv_sem=halo_sems.at[1],
        device_id={"seq": jnp.where(me < n - 1, me + 1, 0)},
        device_id_type=MESH,
    )
    for copy in small:
        copy.wait()

    def parameters(b, carry):
        cols = pl.ds(pl.multiple_of(b * part_width, part_width), part_width)
        c, s = cos_sin_half(ang[:, cols])
        root = jnp.exp(-0.5 * dec[:, cols])
        re, im = square(root * c, root * s)
        r0, r1 = res[0, :, cols], res[1, :, cols]
        tab[RE1, :, cols] = re
        tab[IM1, :, cols] = im
        tab[C1, :, cols] = 2.0 * re
        size = re * re + im * im
        tab[C2, :, cols] = -size
        tab[INVR, :, cols] = re / size
        tab[INVI, :, cols] = -im / size
        tab[G0, :, cols] = r0
        tab[G1, :, cols] = -(r0 * re + r1 * im)
        tab[H1, :, cols] = -r1
        tab[H0R, :, cols] = r0 * re - r1 * im
        tab[H0I, :, cols] = -(r0 * im + r1 * re)
        power = 1
        while power < rows:
            re, im = square(re, im)
            power *= 2
            if power == steps:
                tab[RE16, :, cols], tab[IM16, :, cols] = re, im
            elif power == 2 * steps:
                tab[RE32, :, cols], tab[IM32, :, cols] = re, im
            elif power == 4 * steps:
                tab[RE64, :, cols], tab[IM64, :, cols] = re, im
            elif power == 8 * steps:
                tab[RE128, :, cols], tab[IM128, :, cols] = re, im
        return carry

    lax.fori_loop(0, kv_parts, parameters, 0)
    first_of_later = jnp.where(has_group_before & is_first, 1, 0)
    pl.semaphore_wait(barrier, members - 1 + group + first_of_later)

    for back in range(1, groups):
        @pl.when(group >= back)
        def _():
            signal(ready.at[back], me - back * members)

    @pl.when(has_group_before & is_first)
    def _():
        signal(halo_ready, me - 1)

    @pl.when(has_group_after & is_last)
    def _():
        pl.semaphore_wait(halo_ready, 1)

    pl.when(me < n - 1)(halo_copy.start)

    sub = lax.broadcasted_iota(jnp.int32, (CHUNKS, WIDE), 0)
    first = sub == 0

    def param(which, pole, cols):
        return jnp.broadcast_to(tab[which, pole : pole + 1, cols], (CHUNKS, WIDE))

    def block(b):
        return pl.ds(pl.multiple_of(b * WIDE, WIDE), WIDE)

    def order(b, projections, buffer):
        for slot, i in enumerate(projections):
            buffer[slot] = jnp.dot(to_chunks[...], xs[i, :, block(b)], preferred_element_type=F32)

    def ordered_blocks(projections, work):
        order(0, projections, even)

        def two(pair, carry):
            b = 2 * pair
            order(b + 1, projections, odd)
            work(b, even)
            order(b + 2, projections, even)
            work(b + 1, odd)
            return carry

        lax.fori_loop(0, blocks // 2 - 1, two, 0)
        order(blocks - 1, projections, odd)
        work(blocks - 2, even)
        work(blocks - 1, odd)

    def short(i, x, cols, edge):
        at = [x[CHUNKS * r : CHUNKS * (r + 1), :] for r in range(steps)]
        before2 = jnp.where(first, edge[0], pltpu.roll(at[steps - 2], 1, 0))
        before1 = jnp.where(first, edge[1], pltpu.roll(at[steps - 1], 1, 0))
        at = [before2, before1] + at
        w = [jnp.broadcast_to(taps[tap, i : i + 1, cols], (CHUNKS, WIDE)) for tap in range(3)]
        return [w[0] * at[r] + w[1] * at[r + 1] + w[2] * at[r + 2] for r in range(steps)]

    def message_place(b):
        owner = b // pieces
        return owner, 2 * (b - owner * pieces)

    def pass_a(b, buffer):
        cols = pl.ds(pl.multiple_of(b * WIDE, WIDE), WIDE)
        key = short(1, buffer.at[0], cols, (0.0, 0.0))
        value = short(2, buffer.at[1], cols, (0.0, 0.0))
        c1 = [param(C1, pole, cols) for pole in range(2)]
        c2 = [param(C2, pole, cols) for pole in range(2)]
        now = [jnp.zeros((CHUNKS, WIDE), F32)] * 2
        old = [jnp.zeros((CHUNKS, WIDE), F32)] * 2
        for r in range(steps):
            p = key[r] * value[r]
            prod[CHUNKS * r : CHUNKS * (r + 1), cols] = p
            for pole in range(2):
                now[pole], old[pole] = (p + c2[pole] * old[pole]) + c1[pole] * now[pole], now[pole]
        for pole in range(2):
            re = now[pole] - param(RE1, pole, cols) * old[pole]
            im = param(IM1, pole, cols) * old[pole]
            for shift, wr, wi in ((1, RE16, IM16), (2, RE32, IM32), (4, RE64, IM64)):
                wr, wi = param(wr, pole, cols), param(wi, pole, cols)
                far = sub >= shift
                pr = jnp.where(far, pltpu.roll(re, shift, 0), 0.0)
                pi = jnp.where(far, pltpu.roll(im, shift, 0), 0.0)
                re, im = re + (wr * pr - wi * pi), im + (wr * pi + wi * pr)
            scan[2 * pole, :, cols] = jnp.where(first, 0.0, pltpu.roll(re, 1, 0))
            scan[2 * pole + 1, :, cols] = jnp.where(first, 0.0, pltpu.roll(im, 1, 0))
            owner, row = message_place(b)
            state[owner, pl.ds(row + pole, 1), :] = re[CHUNKS - 1 : CHUNKS]
            state[owner, pl.ds(half + row + pole, 1), :] = im[CHUNKS - 1 : CHUNKS]

    for part in range(kv_parts):
        kv_copy(part).wait()
    ordered_blocks((1, 2), pass_a)

    pl.when(me > 0)(halo_copy.wait_recv)
    keep = me > 0
    received = halo_recv[...].astype(F32)
    received = jnp.where(keep, received, jnp.zeros_like(received))
    halo[:, 0:half_width] = received[0:8]
    halo[:, half_width:width] = received[8:16]

    def fix(owner, carry):
        cols = pl.ds(pl.multiple_of(owner * quarter, quarter), quarter)
        right = [1.0, 1.0]
        for i in (1, 2):
            x = xs[i, 0:16, cols].astype(F32)
            x0, x1 = x[0:1], x[1:2]
            h0, h1 = halo[2 * i : 2 * i + 1, cols], halo[2 * i + 1 : 2 * i + 2, cols]
            w = [taps[tap, i : i + 1, cols] for tap in range(3)]
            right[0] = right[0] * (w[0] * h0 + w[1] * h1 + w[2] * x0)
            right[1] = right[1] * (w[0] * h1 + w[1] * x0 + w[2] * x1)
        d0 = right[0] - prod[0:1, cols]
        d1 = right[1] - prod[CHUNKS : CHUNKS + 1, cols]
        prod[0:1, cols] = right[0]
        prod[CHUNKS : CHUNKS + 1, cols] = right[1]
        inv_r, inv_i = tab[INVR, :, cols], tab[INVI, :, cols]
        re, im = d0 + inv_r * d1, inv_i * d1
        re, im = inv_r * re - inv_i * im, inv_r * im + inv_i * re
        delta[0, :, cols] = re
        delta[1, :, cols] = im
        wr, wi = tab[RE128, :, cols], tab[IM128, :, cols]
        add = (wr * re - wi * im, wr * im + wi * re)
        for part in range(2):
            for piece in range(pieces):
                row = part * half + 2 * piece
                state[owner, row : row + 2, :] += add[part][:, piece * WIDE : (piece + 1) * WIDE]
        t_send[owner] = state[owner].astype(BF16)
        return carry

    lax.fori_loop(0, members, fix, 0)

    def t_copy(source, target):
        return pltpu.make_async_remote_copy(
            src_ref=t_send.at[target],
            dst_ref=t_in.at[source],
            send_sem=t_ssem.at[target],
            recv_sem=t_rsem.at[source],
            device_id={"seq": base + target},
            device_id_type=MESH,
        )

    def c_copy(source, target):
        return pltpu.make_async_remote_copy(
            src_ref=c_out.at[target],
            dst_ref=c_in.at[source],
            send_sem=c_ssem.at[target],
            recv_sem=c_rsem.at[source],
            device_id={"seq": base + target},
            device_id_type=MESH,
        )

    def g_copy(source, ahead):
        return pltpu.make_async_remote_copy(
            src_ref=g_out,
            dst_ref=g_in.at[source],
            send_sem=g_ssem.at[ahead],
            recv_sem=g_rsem.at[source],
            device_id={"seq": lax.rem(me + ahead * members, n)},
            device_id_type=MESH,
        )

    for step in range(1, members):
        t_copy(place, peer(step)).start()

    q_copy.wait()

    def pass_b(b, buffer):
        cols = block(b)
        edge = (halo[0:1, cols], halo[1:2, cols])
        for r, values in enumerate(short(0, buffer.at[0], cols, edge)):
            query[CHUNKS * r : CHUNKS * (r + 1), cols] = values

    def pass_b2(b, carry):
        cols = pl.ds(pl.multiple_of(b * WIDE, WIDE), WIDE)
        c1 = [param(C1, pole, cols) for pole in range(2)]
        c2 = [param(C2, pole, cols) for pole in range(2)]
        g0 = [param(G0, pole, cols) for pole in range(2)]
        g1 = [param(G1, pole, cols) for pole in range(2)]
        gain = jnp.broadcast_to(skip[:, cols], (CHUNKS, WIDE))
        zero = jnp.zeros((CHUNKS, WIDE), F32)
        now, old, before = [zero] * 2, [zero] * 2, zero
        for r in range(steps):
            p = prod[CHUNKS * r : CHUNKS * (r + 1), cols]
            for pole in range(2):
                fresh = ((g0[pole] * p + g1[pole] * before) + c2[pole] * old[pole]) + c1[pole] * now[pole]
                now[pole], old[pole] = fresh, now[pole]
            local[CHUNKS * r : CHUNKS * (r + 1), cols] = now[0] + now[1] + gain * p
            before = p
        return carry

    ordered_blocks((0,), pass_b)

    t_in[pl.ds(place, 1)] = t_send[pl.ds(place, 1)]
    for piece in range(pieces):
        cols = pl.ds(pl.multiple_of(place * quarter + piece * WIDE, WIDE), WIDE)
        spin[0, 2 * piece : 2 * piece + 2, :] = tab[RE128, :, cols]
        spin[1, 2 * piece : 2 * piece + 2, :] = tab[IM128, :, cols]
    for step in range(1, members):
        t_copy(peer(step), place).wait_recv()

    wr, wi = spin[0], spin[1]
    re = im = jnp.zeros((half, WIDE), F32)
    inside = []
    for member in range(members):
        inside.append((re, im))
        ended = t_in[member].astype(F32)
        re, im = wr * re - wi * im + ended[:half], wr * im + wi * re + ended[half:]
    g_out[...] = jnp.concatenate([re, im], axis=0).astype(BF16)

    def send_g(ahead):
        pl.semaphore_wait(ready.at[ahead], 1)
        g_copy(group, ahead).start()

    in_later_groups(send_g)

    gr, gi = wr, wi
    span = 1
    while span < members:
        gr, gi = square(gr, gi)
        span *= 2

    def add_group(source, state):
        re, im = state
        g_copy(source, 1).wait_recv()
        ended = g_in[source].astype(F32)
        return gr * re - gi * im + ended[:half], gr * im + gi * re + ended[half:]

    zero = jnp.zeros((half, WIDE), F32)
    re, im = lax.fori_loop(0, group, add_group, (zero, zero))
    for member in range(members):
        c_out[member] = jnp.concatenate(
            [inside[member][0] + re, inside[member][1] + im], axis=0
        ).astype(BF16)
        re, im = wr * re - wi * im, wr * im + wi * re

    for step in range(1, members):
        c_copy(place, peer(step)).start()
    c_in[pl.ds(place, 1)] = c_out[pl.ds(place, 1)]

    lax.fori_loop(0, blocks, pass_b2, 0, unroll=2)

    for step in range(1, members):
        c_copy(peer(step), place).wait_recv()
    carried[...] = c_in[...].astype(F32)

    def out_copy(b):
        cols = pl.ds(pl.multiple_of(b * WIDE, WIDE), WIDE)
        return pltpu.make_async_copy(outs.at[:, cols], out_hbm.at[:, cols], out_sems.at[b])

    def pass_c(b, buffer):
        cols = pl.ds(pl.multiple_of(b * WIDE, WIDE), WIDE)
        c1 = [param(C1, pole, cols) for pole in range(2)]
        c2 = [param(C2, pole, cols) for pole in range(2)]
        now, old = [], []
        for pole in range(2):
            owner, row = message_place(b)
            cr = jnp.broadcast_to(carried[owner, pl.ds(row + pole, 1), :], (CHUNKS, WIDE))
            ci = jnp.broadcast_to(carried[owner, pl.ds(half + row + pole, 1), :], (CHUNKS, WIDE))
            dr = jnp.broadcast_to(delta[0, pole : pole + 1, cols], (CHUNKS, WIDE))
            di = jnp.broadcast_to(delta[1, pole : pole + 1, cols], (CHUNKS, WIDE))
            cr, ci = jnp.where(first, cr, cr + dr), jnp.where(first, ci, ci + di)
            for bit, wr, wi in ((1, RE16, IM16), (2, RE32, IM32), (4, RE64, IM64)):
                wr, wi = param(wr, pole, cols), param(wi, pole, cols)
                has = (sub & bit) > 0
                cr, ci = (
                    jnp.where(has, wr * cr - wi * ci, cr),
                    jnp.where(has, wr * ci + wi * cr, ci),
                )
            zr = scan[2 * pole, :, cols] + cr
            zi = scan[2 * pole + 1, :, cols] + ci
            old.append(param(G0, pole, cols) * zr + param(H1, pole, cols) * zi)
            now.append(param(H0R, pole, cols) * zr + param(H0I, pole, cols) * zi)
        done = []
        for r in range(steps):
            at = slice(CHUNKS * r, CHUNKS * (r + 1))
            done.append(query[at, cols] * (local[at, cols] + (now[0] + now[1])))
            for pole in range(2):
                now[pole], old[pole] = c2[pole] * old[pole] + c1[pole] * now[pole], now[pole]
        buffer[...] = jnp.concatenate(done, axis=0).astype(BF16)

    def give(b, buffer):
        outs[:, block(b)] = jnp.dot(
            to_rows[...], buffer[...], preferred_element_type=F32
        ).astype(BF16)
        out_copy(b).start()

    pass_c(0, gated_even)

    def two_out(pair, carry):
        b = 2 * pair
        pass_c(b + 1, gated_odd)
        give(b, gated_even)
        pass_c(b + 2, gated_even)
        give(b + 1, gated_odd)
        return carry

    lax.fori_loop(0, blocks // 2 - 1, two_out, 0)
    pass_c(blocks - 1, gated_odd)
    give(blocks - 2, gated_even)
    give(blocks - 1, gated_odd)

    def wait_out(b, carry):
        out_copy(b).wait()
        return carry

    lax.fori_loop(0, blocks, wait_out, 0)

    for step in range(1, members):
        t_copy(place, peer(step)).wait_send()
        c_copy(place, peer(step)).wait_send()
    in_later_groups(lambda ahead: g_copy(group, ahead).wait_send())
    pl.when(me < n - 1)(halo_copy.wait_send)


def solution(mesh):
    n = mesh.shape["seq"]

    def on_device(projected, short_taps, skip_gain, residues, pole_angles, decay_rates):
        _, rows, width = projected.shape
        members = math.gcd(n, 4)
        quarter = width // members
        groups = n // members
        message = 4 * quarter // WIDE
        kv_parts = 4
        dma = pltpu.SemaphoreType.DMA
        vmem = pltpu.VMEM
        return pl.pallas_call(
            functools.partial(kernel, n, members),
            out_shape=pltpu.VMEM((rows, width), BF16),
            in_specs=[pl.BlockSpec(memory_space=pl.ANY)] * 6,
            out_specs=pl.BlockSpec(memory_space=pl.ANY),
            scratch_shapes=[
                vmem((3, rows, width), BF16),
                vmem((2, rows, WIDE), F32),
                vmem((2, rows, WIDE), F32),
                vmem((rows, WIDE), BF16),
                vmem((rows, WIDE), BF16),
                vmem((2, 2, width), F32),
                vmem((3, 16, width), BF16),
                vmem(short_taps.shape, F32),
                vmem((1, width), F32),
                vmem(residues.shape, F32),
                vmem(pole_angles.shape, F32),
                vmem(decay_rates.shape, F32),
                vmem((rows, rows), BF16),
                vmem((rows, rows), BF16),
                vmem((TABLE_ROWS, 2, width), F32),
                vmem((16, width // 2), F32),
                vmem((16, width // 2), BF16),
                vmem((16, width // 2), BF16),
                vmem((8, width), F32),
                vmem((rows, width), F32),
                vmem((rows, width), F32),
                vmem((rows, width), F32),
                vmem((4, CHUNKS, width), F32),
                vmem((members, message, WIDE), F32),
                vmem((2, message // 2, WIDE), F32),
                vmem((members, message, WIDE), F32),
                vmem((members, message, WIDE), BF16),
                vmem((members, message, WIDE), BF16),
                vmem((members, message, WIDE), BF16),
                vmem((members, message, WIDE), BF16),
                vmem((message, WIDE), BF16),
                vmem((groups, message, WIDE), BF16),
                vmem((rows, width), BF16),
                dma((7,)),
                dma((kv_parts,)),
                dma((width // WIDE,)),
                dma((2,)),
                dma((members,)),
                dma((members,)),
                dma((members,)),
                dma((members,)),
                dma((groups,)),
                dma((groups,)),
                pltpu.SemaphoreType.REGULAR((groups,)),
                pltpu.SemaphoreType.REGULAR,
            ],
            compiler_params=pltpu.CompilerParams(
                collective_id=0, has_side_effects=True, vmem_limit_bytes=40 * 1024 * 1024
            ),
            cost_estimate=pl.CostEstimate(
                flops=60 * rows * width, bytes_accessed=8 * rows * width, transcendentals=2 * width
            ),
        )(
            *[
                pltpu.with_memory_space_constraint(x, pltpu.HBM)
                for x in (
                    projected, short_taps, skip_gain.reshape(1, width), residues, pole_angles, decay_rates
                )
            ]
        )

    return jax.shard_map(
        on_device,
        mesh=mesh,
        in_specs=(P(None, ("grp", "seq"), None), P(), P(), P(), P(), P()),
        out_specs=P(("grp", "seq"), None),
        check_vma=False,
    )
```

```python
import functools
import math

import jax
import jax.numpy as jnp
from jax import lax
from jax.experimental import pallas as pl
from jax.experimental.pallas import tpu as pltpu
from jax.sharding import PartitionSpec as P

MESH = pl.DeviceIdType.MESH
CHUNKS = 8
WIDE = 256
F32 = jnp.float32
BF16 = jnp.bfloat16

RE1, IM1, C1, C2, RE16, IM16, RE32, IM32, RE64, IM64, RE128, IM128, G0, G1, H1, H0R, H0I, INVR, INVI = range(19)
TABLE_ROWS = 19


def square(re, im):
    return re * re - im * im, 2.0 * (re * im)


def cos_sin_half(angle):
    x = 0.5 * angle
    z = x * x
    s = 1.0 / 6227020800.0
    for coefficient in (-1.0 / 39916800.0, 1.0 / 362880.0, -1.0 / 5040.0, 1.0 / 120.0, -1.0 / 6.0, 1.0):
        s = s * z + coefficient
    c = -1.0 / 87178291200.0
    for coefficient in (1.0 / 479001600.0, -1.0 / 3628800.0, 1.0 / 40320.0, -1.0 / 720.0, 1.0 / 24.0, -0.5, 1.0):
        c = c * z + coefficient
    return c, s * x


def kernel(
    n, members,
    x_hbm, taps_hbm, skip_hbm, res_hbm, ang_hbm, dec_hbm, out_hbm,
    xs, even, odd, gated_even, gated_odd, delta, tail, taps, skip, res, ang, dec, to_chunks, to_rows, tab,
    halo_f32, halo_send, halo_recv, halo,
    prod, local, query, scan, state, spin, carried, t_send, t_in, c_out, c_in, g_out, g_in, outs,
    in_sems, kv_sems, out_sems, halo_sems, t_ssem, t_rsem, c_ssem, c_rsem, g_ssem, g_rsem, ready, halo_ready,
):
    rows, width = xs.shape[1], xs.shape[2]
    steps = rows // CHUNKS
    half_width = width // 2
    blocks = width // WIDE
    kv_parts = kv_sems.shape[0]
    part_width = width // kv_parts
    quarter = width // members
    pieces = quarter // WIDE
    half = 2 * pieces
    me = lax.axis_index("seq")
    place = lax.rem(me, members)
    base = me - place
    groups = n // members
    group = base // members
    has_group_before = base > 0
    has_group_after = base + members < n
    is_first = place == 0
    is_last = place == members - 1

    def peer(step):
        other = place + step
        return jnp.where(other >= members, other - members, other)

    barrier = pltpu.get_barrier_semaphore()

    def signal(semaphore, device):
        pl.semaphore_signal(semaphore, inc=1, device_id={"seq": device}, device_id_type=MESH)

    for step in range(1, members):
        signal(barrier, base + peer(step))

    def in_later_groups(action):
        for ahead in range(1, groups):
            pl.when(group + ahead < groups)(functools.partial(action, ahead))

    in_later_groups(lambda ahead: signal(barrier, me + ahead * members))

    @pl.when(has_group_after & is_last)
    def _():
        signal(barrier, me + 1)

    def kv_copy(part):
        cols = pl.ds(pl.multiple_of(part * part_width, part_width), part_width)
        return pltpu.make_async_copy(
            x_hbm.at[pl.ds(1, 2), :, cols], xs.at[pl.ds(1, 2), :, cols], kv_sems.at[part]
        )

    tail_copy = pltpu.make_async_copy(
        x_hbm.at[:, pl.ds(rows - 16, 16), :], tail, in_sems.at[0]
    )
    tail_copy.start()
    small = [
        pltpu.make_async_copy(source, target, in_sems.at[1 + i])
        for i, (source, target) in enumerate(
            [(ang_hbm, ang), (dec_hbm, dec), (res_hbm, res), (taps_hbm, taps), (skip_hbm, skip)]
        )
    ]
    for copy in small:
        copy.start()
    for part in range(kv_parts):
        kv_copy(part).start()
    q_copy = pltpu.make_async_copy(x_hbm.at[0], xs.at[0], in_sems.at[6])
    q_copy.start()

    i0 = lax.broadcasted_iota(jnp.int32, (rows, rows), 0)
    i1 = lax.broadcasted_iota(jnp.int32, (rows, rows), 1)
    to_chunks[...] = jnp.where(i1 == (i0 & (CHUNKS - 1)) * steps + (i0 >> 3), 1.0, 0.0).astype(BF16)

    to_rows[...] = jnp.where(i0 == (i1 & (CHUNKS - 1)) * steps + (i1 >> 3), 1.0, 0.0).astype(BF16)

    tail_copy.wait()
    for i in range(3):
        last = tail[i].astype(F32)[14:16]
        halo_f32[2 * i : 2 * i + 2, :] = last[:, :half_width]
        halo_f32[8 + 2 * i : 10 + 2 * i, :] = last[:, half_width:]
    halo_f32[6:8, :] = jnp.zeros((2, half_width), F32)
    halo_f32[14:16, :] = jnp.zeros((2, half_width), F32)
    halo_send[...] = halo_f32[...].astype(BF16)
    halo_copy = pltpu.make_async_remote_copy(
        src_ref=halo_send,
        dst_ref=halo_recv,
        send_sem=halo_sems.at[0],
        recv_sem=halo_sems.at[1],
        device_id={"seq": jnp.where(me < n - 1, me + 1, 0)},
        device_id_type=MESH,
    )
    for copy in small:
        copy.wait()

    def parameters(b, carry):
        cols = pl.ds(pl.multiple_of(b * part_width, part_width), part_width)
        c, s = cos_sin_half(ang[:, cols])
        root = jnp.exp(-0.5 * dec[:, cols])
        re, im = square(root * c, root * s)
        r0, r1 = res[0, :, cols], res[1, :, cols]
        tab[RE1, :, cols] = re
        tab[IM1, :, cols] = im
        tab[C1, :, cols] = 2.0 * re
        size = re * re + im * im
        tab[C2, :, cols] = -size
        tab[INVR, :, cols] = re / size
        tab[INVI, :, cols] = -im / size
        tab[G0, :, cols] = r0
        tab[G1, :, cols] = -(r0 * re + r1 * im)
        tab[H1, :, cols] = -r1
        tab[H0R, :, cols] = r0 * re - r1 * im
        tab[H0I, :, cols] = -(r0 * im + r1 * re)
        power = 1
        while power < rows:
            re, im = square(re, im)
            power *= 2
            if power == steps:
                tab[RE16, :, cols], tab[IM16, :, cols] = re, im
            elif power == 2 * steps:
                tab[RE32, :, cols], tab[IM32, :, cols] = re, im
            elif power == 4 * steps:
                tab[RE64, :, cols], tab[IM64, :, cols] = re, im
            elif power == 8 * steps:
                tab[RE128, :, cols], tab[IM128, :, cols] = re, im
        return carry

    lax.fori_loop(0, kv_parts, parameters, 0)
    first_of_later = jnp.where(has_group_before & is_first, 1, 0)
    pl.semaphore_wait(barrier, members - 1 + group + first_of_later)

    for back in range(1, groups):
        @pl.when(group >= back)
        def _():
            signal(ready.at[back], me - back * members)

    @pl.when(has_group_before & is_first)
    def _():
        signal(halo_ready, me - 1)

    @pl.when(has_group_after & is_last)
    def _():
        pl.semaphore_wait(halo_ready, 1)

    pl.when(me < n - 1)(halo_copy.start)

    sub = lax.broadcasted_iota(jnp.int32, (CHUNKS, WIDE), 0)
    first = sub == 0

    def param(which, pole, cols):
        return jnp.broadcast_to(tab[which, pole : pole + 1, cols], (CHUNKS, WIDE))

    def block(b):
        return pl.ds(pl.multiple_of(b * WIDE, WIDE), WIDE)

    def order(b, projections, buffer):
        for slot, i in enumerate(projections):
            buffer[slot] = jnp.dot(to_chunks[...], xs[i, :, block(b)], preferred_element_type=F32)

    def ordered_blocks(projections, work, start, stop):
        order(start, projections, even)

        def two(pair, carry):
            b = start + 2 * pair
            order(b + 1, projections, odd)
            work(b, even)
            order(b + 2, projections, even)
            work(b + 1, odd)
            return carry

        lax.fori_loop(0, (stop - start) // 2 - 1, two, 0)
        order(stop - 1, projections, odd)
        work(stop - 2, even)
        work(stop - 1, odd)

    def short(i, x, cols, edge):
        at = [x[CHUNKS * r : CHUNKS * (r + 1), :] for r in range(steps)]
        before2 = jnp.where(first, edge[0], pltpu.roll(at[steps - 2], 1, 0))
        before1 = jnp.where(first, edge[1], pltpu.roll(at[steps - 1], 1, 0))
        at = [before2, before1] + at
        w = [jnp.broadcast_to(taps[tap, i : i + 1, cols], (CHUNKS, WIDE)) for tap in range(3)]
        return [w[0] * at[r] + w[1] * at[r + 1] + w[2] * at[r + 2] for r in range(steps)]

    def message_place(b):
        owner = b // pieces
        return owner, 2 * (b - owner * pieces)

    def pass_a(b, buffer):
        cols = pl.ds(pl.multiple_of(b * WIDE, WIDE), WIDE)
        key = short(1, buffer.at[0], cols, (0.0, 0.0))
        value = short(2, buffer.at[1], cols, (0.0, 0.0))
        c1 = [param(C1, pole, cols) for pole in range(2)]
        c2 = [param(C2, pole, cols) for pole in range(2)]
        now = [jnp.zeros((CHUNKS, WIDE), F32)] * 2
        old = [jnp.zeros((CHUNKS, WIDE), F32)] * 2
        for r in range(steps):
            p = key[r] * value[r]
            prod[CHUNKS * r : CHUNKS * (r + 1), cols] = p
            for pole in range(2):
                now[pole], old[pole] = (p + c2[pole] * old[pole]) + c1[pole] * now[pole], now[pole]
        for pole in range(2):
            re = now[pole] - param(RE1, pole, cols) * old[pole]
            im = param(IM1, pole, cols) * old[pole]
            for shift, wr, wi in ((1, RE16, IM16), (2, RE32, IM32), (4, RE64, IM64)):
                wr, wi = param(wr, pole, cols), param(wi, pole, cols)
                far = sub >= shift
                pr = jnp.where(far, pltpu.roll(re, shift, 0), 0.0)
                pi = jnp.where(far, pltpu.roll(im, shift, 0), 0.0)
                re, im = re + (wr * pr - wi * pi), im + (wr * pi + wi * pr)
            scan[2 * pole, :, cols] = jnp.where(first, 0.0, pltpu.roll(re, 1, 0))
            scan[2 * pole + 1, :, cols] = jnp.where(first, 0.0, pltpu.roll(im, 1, 0))
            owner, row = message_place(b)
            state[owner, pl.ds(row + pole, 1), :] = re[CHUNKS - 1 : CHUNKS]
            state[owner, pl.ds(half + row + pole, 1), :] = im[CHUNKS - 1 : CHUNKS]

    for part in range(kv_parts):
        kv_copy(part).wait()
    ordered_blocks((1, 2), pass_a, 0, blocks)

    pl.when(me > 0)(halo_copy.wait_recv)
    keep = me > 0
    received = halo_recv[...].astype(F32)
    received = jnp.where(keep, received, jnp.zeros_like(received))
    halo[:, 0:half_width] = received[0:8]
    halo[:, half_width:width] = received[8:16]

    def fix(owner, carry):
        cols = pl.ds(pl.multiple_of(owner * quarter, quarter), quarter)
        right = [1.0, 1.0]
        for i in (1, 2):
            x = xs[i, 0:16, cols].astype(F32)
            x0, x1 = x[0:1], x[1:2]
            h0, h1 = halo[2 * i : 2 * i + 1, cols], halo[2 * i + 1 : 2 * i + 2, cols]
            w = [taps[tap, i : i + 1, cols] for tap in range(3)]
            right[0] = right[0] * (w[0] * h0 + w[1] * h1 + w[2] * x0)
            right[1] = right[1] * (w[0] * h1 + w[1] * x0 + w[2] * x1)
        d0 = right[0] - prod[0:1, cols]
        d1 = right[1] - prod[CHUNKS : CHUNKS + 1, cols]
        prod[0:1, cols] = right[0]
        prod[CHUNKS : CHUNKS + 1, cols] = right[1]
        inv_r, inv_i = tab[INVR, :, cols], tab[INVI, :, cols]
        re, im = d0 + inv_r * d1, inv_i * d1
        re, im = inv_r * re - inv_i * im, inv_r * im + inv_i * re
        delta[0, :, cols] = re
        delta[1, :, cols] = im
        wr, wi = tab[RE128, :, cols], tab[IM128, :, cols]
        add = (wr * re - wi * im, wr * im + wi * re)
        for part in range(2):
            for piece in range(pieces):
                row = part * half + 2 * piece
                state[owner, row : row + 2, :] += add[part][:, piece * WIDE : (piece + 1) * WIDE]
        t_send[owner] = state[owner].astype(BF16)
        return carry

    lax.fori_loop(0, members, fix, 0)

    def t_copy(source, target):
        return pltpu.make_async_remote_copy(
            src_ref=t_send.at[target],
            dst_ref=t_in.at[source],
            send_sem=t_ssem.at[target],
            recv_sem=t_rsem.at[source],
            device_id={"seq": base + target},
            device_id_type=MESH,
        )

    def c_copy(source, target):
        return pltpu.make_async_remote_copy(
            src_ref=c_out.at[target],
            dst_ref=c_in.at[source],
            send_sem=c_ssem.at[target],
            recv_sem=c_rsem.at[source],
            device_id={"seq": base + target},
            device_id_type=MESH,
        )

    def g_copy(source, ahead):
        return pltpu.make_async_remote_copy(
            src_ref=g_out,
            dst_ref=g_in.at[source],
            send_sem=g_ssem.at[ahead],
            recv_sem=g_rsem.at[source],
            device_id={"seq": lax.rem(me + ahead * members, n)},
            device_id_type=MESH,
        )

    for step in range(1, members):
        t_copy(place, peer(step)).start()

    q_copy.wait()

    def pass_b(b, buffer):
        cols = block(b)
        edge = (halo[0:1, cols], halo[1:2, cols])
        for r, values in enumerate(short(0, buffer.at[0], cols, edge)):
            query[CHUNKS * r : CHUNKS * (r + 1), cols] = values

    def pass_b2(b, carry):
        cols = pl.ds(pl.multiple_of(b * WIDE, WIDE), WIDE)
        c1 = [param(C1, pole, cols) for pole in range(2)]
        c2 = [param(C2, pole, cols) for pole in range(2)]
        g0 = [param(G0, pole, cols) for pole in range(2)]
        g1 = [param(G1, pole, cols) for pole in range(2)]
        gain = jnp.broadcast_to(skip[:, cols], (CHUNKS, WIDE))
        zero = jnp.zeros((CHUNKS, WIDE), F32)
        now, old, before = [zero] * 2, [zero] * 2, zero
        for r in range(steps):
            p = prod[CHUNKS * r : CHUNKS * (r + 1), cols]
            for pole in range(2):
                fresh = ((g0[pole] * p + g1[pole] * before) + c2[pole] * old[pole]) + c1[pole] * now[pole]
                now[pole], old[pole] = fresh, now[pole]
            local[CHUNKS * r : CHUNKS * (r + 1), cols] = now[0] + now[1] + gain * p
            before = p
        return carry

    ordered_blocks((0,), pass_b, 0, blocks // 2)

    t_in[pl.ds(place, 1)] = t_send[pl.ds(place, 1)]
    for piece in range(pieces):
        cols = pl.ds(pl.multiple_of(place * quarter + piece * WIDE, WIDE), WIDE)
        spin[0, 2 * piece : 2 * piece + 2, :] = tab[RE128, :, cols]
        spin[1, 2 * piece : 2 * piece + 2, :] = tab[IM128, :, cols]
    for step in range(1, members):
        t_copy(peer(step), place).wait_recv()

    wr, wi = spin[0], spin[1]
    re = im = jnp.zeros((half, WIDE), F32)
    inside = []
    for member in range(members):
        inside.append((re, im))
        ended = t_in[member].astype(F32)
        re, im = wr * re - wi * im + ended[:half], wr * im + wi * re + ended[half:]
    g_out[...] = jnp.concatenate([re, im], axis=0).astype(BF16)

    def send_g(ahead):
        pl.semaphore_wait(ready.at[ahead], 1)
        g_copy(group, ahead).start()

    in_later_groups(send_g)
    ordered_blocks((0,), pass_b, blocks // 2, blocks)

    gr, gi = wr, wi
    span = 1
    while span < members:
        gr, gi = square(gr, gi)
        span *= 2

    def add_group(source, state):
        re, im = state
        g_copy(source, 1).wait_recv()
        ended = g_in[source].astype(F32)
        return gr * re - gi * im + ended[:half], gr * im + gi * re + ended[half:]

    zero = jnp.zeros((half, WIDE), F32)
    re, im = lax.fori_loop(0, group, add_group, (zero, zero))
    for member in range(members):
        c_out[member] = jnp.concatenate(
            [inside[member][0] + re, inside[member][1] + im], axis=0
        ).astype(BF16)
        re, im = wr * re - wi * im, wr * im + wi * re

    for step in range(1, members):
        c_copy(place, peer(step)).start()
    c_in[pl.ds(place, 1)] = c_out[pl.ds(place, 1)]

    lax.fori_loop(0, blocks, pass_b2, 0, unroll=2)

    for step in range(1, members):
        c_copy(peer(step), place).wait_recv()
    carried[...] = c_in[...].astype(F32)

    def out_copy(b):
        cols = pl.ds(pl.multiple_of(b * WIDE, WIDE), WIDE)
        return pltpu.make_async_copy(outs.at[:, cols], out_hbm.at[:, cols], out_sems.at[b])

    def pass_c(b, buffer):
        cols = pl.ds(pl.multiple_of(b * WIDE, WIDE), WIDE)
        c1 = [param(C1, pole, cols) for pole in range(2)]
        c2 = [param(C2, pole, cols) for pole in range(2)]
        now, old = [], []
        for pole in range(2):
            owner, row = message_place(b)
            cr = jnp.broadcast_to(carried[owner, pl.ds(row + pole, 1), :], (CHUNKS, WIDE))
            ci = jnp.broadcast_to(carried[owner, pl.ds(half + row + pole, 1), :], (CHUNKS, WIDE))
            dr = jnp.broadcast_to(delta[0, pole : pole + 1, cols], (CHUNKS, WIDE))
            di = jnp.broadcast_to(delta[1, pole : pole + 1, cols], (CHUNKS, WIDE))
            cr, ci = jnp.where(first, cr, cr + dr), jnp.where(first, ci, ci + di)
            for bit, wr, wi in ((1, RE16, IM16), (2, RE32, IM32), (4, RE64, IM64)):
                wr, wi = param(wr, pole, cols), param(wi, pole, cols)
                has = (sub & bit) > 0
                cr, ci = (
                    jnp.where(has, wr * cr - wi * ci, cr),
                    jnp.where(has, wr * ci + wi * cr, ci),
                )
            zr = scan[2 * pole, :, cols] + cr
            zi = scan[2 * pole + 1, :, cols] + ci
            old.append(param(G0, pole, cols) * zr + param(H1, pole, cols) * zi)
            now.append(param(H0R, pole, cols) * zr + param(H0I, pole, cols) * zi)
        done = []
        for r in range(steps):
            at = slice(CHUNKS * r, CHUNKS * (r + 1))
            done.append(query[at, cols] * (local[at, cols] + (now[0] + now[1])))
            for pole in range(2):
                now[pole], old[pole] = c2[pole] * old[pole] + c1[pole] * now[pole], now[pole]
        buffer[...] = jnp.concatenate(done, axis=0).astype(BF16)

    def give(b, buffer):
        outs[:, block(b)] = jnp.dot(
            to_rows[...], buffer[...], preferred_element_type=F32
        ).astype(BF16)
        out_copy(b).start()

    pass_c(0, gated_even)

    def two_out(pair, carry):
        b = 2 * pair
        pass_c(b + 1, gated_odd)
        give(b, gated_even)
        pass_c(b + 2, gated_even)
        give(b + 1, gated_odd)
        return carry

    lax.fori_loop(0, blocks // 2 - 1, two_out, 0)
    pass_c(blocks - 1, gated_odd)
    give(blocks - 2, gated_even)
    give(blocks - 1, gated_odd)

    def wait_out(b, carry):
        out_copy(b).wait()
        return carry

    lax.fori_loop(0, blocks, wait_out, 0)

    for step in range(1, members):
        t_copy(place, peer(step)).wait_send()
        c_copy(place, peer(step)).wait_send()
    in_later_groups(lambda ahead: g_copy(group, ahead).wait_send())
    pl.when(me < n - 1)(halo_copy.wait_send)


def solution(mesh):
    n = mesh.shape["seq"]

    def on_device(projected, short_taps, skip_gain, residues, pole_angles, decay_rates):
        _, rows, width = projected.shape
        members = math.gcd(n, 4)
        quarter = width // members
        groups = n // members
        message = 4 * quarter // WIDE
        kv_parts = 4
        dma = pltpu.SemaphoreType.DMA
        vmem = pltpu.VMEM
        return pl.pallas_call(
            functools.partial(kernel, n, members),
            out_shape=pltpu.VMEM((rows, width), BF16),
            in_specs=[pl.BlockSpec(memory_space=pl.ANY)] * 6,
            out_specs=pl.BlockSpec(memory_space=pl.ANY),
            scratch_shapes=[
                vmem((3, rows, width), BF16),
                vmem((2, rows, WIDE), F32),
                vmem((2, rows, WIDE), F32),
                vmem((rows, WIDE), BF16),
                vmem((rows, WIDE), BF16),
                vmem((2, 2, width), F32),
                vmem((3, 16, width), BF16),
                vmem(short_taps.shape, F32),
                vmem((1, width), F32),
                vmem(residues.shape, F32),
                vmem(pole_angles.shape, F32),
                vmem(decay_rates.shape, F32),
                vmem((rows, rows), BF16),
                vmem((rows, rows), BF16),
                vmem((TABLE_ROWS, 2, width), F32),
                vmem((16, width // 2), F32),
                vmem((16, width // 2), BF16),
                vmem((16, width // 2), BF16),
                vmem((8, width), F32),
                vmem((rows, width), F32),
                vmem((rows, width), F32),
                vmem((rows, width), F32),
                vmem((4, CHUNKS, width), F32),
                vmem((members, message, WIDE), F32),
                vmem((2, message // 2, WIDE), F32),
                vmem((members, message, WIDE), F32),
                vmem((members, message, WIDE), BF16),
                vmem((members, message, WIDE), BF16),
                vmem((members, message, WIDE), BF16),
                vmem((members, message, WIDE), BF16),
                vmem((message, WIDE), BF16),
                vmem((groups, message, WIDE), BF16),
                vmem((rows, width), BF16),
                dma((7,)),
                dma((kv_parts,)),
                dma((width // WIDE,)),
                dma((2,)),
                dma((members,)),
                dma((members,)),
                dma((members,)),
                dma((members,)),
                dma((groups,)),
                dma((groups,)),
                pltpu.SemaphoreType.REGULAR((groups,)),
                pltpu.SemaphoreType.REGULAR,
            ],
            compiler_params=pltpu.CompilerParams(
                collective_id=0, has_side_effects=True, vmem_limit_bytes=40 * 1024 * 1024
            ),
            cost_estimate=pl.CostEstimate(
                flops=60 * rows * width, bytes_accessed=8 * rows * width, transcendentals=2 * width
            ),
        )(
            *[
                pltpu.with_memory_space_constraint(x, pltpu.HBM)
                for x in (
                    projected, short_taps, skip_gain.reshape(1, width), residues, pole_angles, decay_rates
                )
            ]
        )

    return jax.shard_map(
        on_device,
        mesh=mesh,
        in_specs=(P(None, ("grp", "seq"), None), P(), P(), P(), P(), P()),
        out_specs=P(("grp", "seq"), None),
        check_vma=False,
    )
```
